32 devices in a mesh: seq: 8 (over z, core), hid: 4 (over y, x).
Axes of the slice: x: 2, y: 2, z: 4, core: 2. Of those that a mesh axis runs over, the one named last changes fastest.
Arguments:
- activations: bfloat16 [4096, 4096], P('seq'), may hold values from -6 to 6
- w_inner: bfloat16 [4096, 4096], P('seq', 'hid'), may hold values from -0.09375 to 0.09375
- w_gate: bfloat16 [4096, 4096], P('seq', 'hid'), may hold values from -0.09375 to 0.09375
- w_groups: bfloat16 [4096, 1024], P('seq'), may hold values from -0.09375 to 0.09375
- w_step: bfloat16 [4096, 64], P('seq'), may hold values from -0.09375 to 0.09375
- w_out: bfloat16 [4096, 4096], P('seq', 'hid'), may hold values from -0.09375 to 0.09375
- conv_inner: float32 [4, 4096], P(None, 'hid'), may hold values from -3 to 3
- conv_groups: float32 [4, 1024], replicated, may hold values from -3 to 3
- step_bias: float32 [64], P('hid'), may hold values from -4 to 0
- decay_log: float32 [64], P('hid'), may hold values from -9 to -1
- skip_gain: float32 [64], P('hid'), may hold values from 0.5 to 1.5
- norm_gain: float32 [4096], P('hid'), may hold values from 0.5 to 1.5
Outputs:
- layer_out: bfloat16 [4096, 4096], P('seq', 'hid')
The draws below stay inside these ranges and needn't reach their ends.
All inputs are finite; a program needn't handle non-finite values.
Results may differ from the reference program's by a relative error of at most 0.02.
Values may be sent and summed in bfloat16 or wider, within the bound.
No kernel may reach another device: no remote copies, remote signals or barrier semaphores. Data moves between devices by JAX's collectives and lax.ppermute only.
A program may use at most 128 MiB of HBM per device.

```python
import jax
import jax.numpy as jnp
from jax import lax

D = 4096
HEADS = 64
P_SIZE = 64
N = 128
G = 4
Q = 256
K = 4
INNER = 4096
TOKENS = 4096
N_HID = 4


def block_scale(own_key, extent, pieces, low, high):
    loudness = 1.0
    for dim, shards_of in pieces:
        heights = jax.random.uniform(jax.random.fold_in(jax.random.fold_in(own_key, 6), dim), (shards_of,), jnp.float32, low / len(pieces), high / len(pieces))
        loudness = loudness * jnp.repeat(jnp.exp(heights), extent[dim] // shards_of).reshape((-1,) + (1,) * (len(extent) - 1 - dim))
    return loudness


def normal_values(stream_key, dims, width, limit, pieces=(), dtype=jnp.bfloat16):
    level = block_scale(stream_key, dims, pieces, -0.22, 0.18) if pieces else 1.0
    array = jax.random.normal(stream_key, dims, jnp.float32) * width * level
    return jnp.minimum(jnp.maximum(array, -limit), limit).astype(dtype)


def setup_inputs(seed: int = 0) -> dict:
    key_of = jax.random.split(jax.random.key(seed), 13)
    return {
        "activations": normal_values(key_of[0], (TOKENS, D), 1.0, 6.0, ((0, 8),)),
        "w_inner": normal_values(key_of[1], (D, INNER), D ** -0.5, 0.09375, ((0, 8), (1, 4))),
        "w_gate": normal_values(key_of[2], (D, INNER), D ** -0.5, 0.09375, ((0, 8), (1, 4))),
        "w_groups": normal_values(key_of[3], (D, 2 * G * N), D ** -0.5, 0.09375, ((0, 8),)),
        "w_step": normal_values(key_of[4], (D, HEADS), D ** -0.5, 0.09375, ((0, 8),)),
        "w_out": normal_values(key_of[5], (D, INNER), INNER ** -0.5, 0.09375, ((0, 8), (1, 4))),
        "conv_inner": normal_values(key_of[6], (K, INNER), 0.5, 3.0, ((1, 4),), jnp.float32),
        "conv_groups": normal_values(key_of[7], (K, 2 * G * N), 0.5, 3.0, (), jnp.float32),
        "step_bias": jnp.clip(-4.0 + 4.0 * jax.random.uniform(key_of[8], (HEADS,), jnp.float32) ** block_scale(key_of[8], (HEADS,), ((0, 4),), -0.2, 0.2), -4.0, 0.0),
        "decay_log": jnp.clip(-9.0 + 8.0 * jax.random.uniform(key_of[9], (HEADS,), jnp.float32) ** block_scale(key_of[9], (HEADS,), ((0, 4),), -0.2, 0.2), -9.0, -1.0),
        "skip_gain": jnp.clip(0.5 + 1.0 * jax.random.uniform(key_of[10], (HEADS,), jnp.float32) ** block_scale(key_of[10], (HEADS,), ((0, 4),), -0.2, 0.2), 0.5, 1.5),
        "norm_gain": jnp.clip(1.0 + 0.1 * jax.random.normal(key_of[11], (INNER,), jnp.float32), 0.5, 1.5),
    }


def causal_conv(values, kernel):
    tap_count = kernel.shape[0]
    length = values.shape[0]
    padded = jnp.pad(values.astype(jnp.float32), ((tap_count - 1, 0), (0, 0)))
    summed = jnp.zeros(values.shape, jnp.float32)
    for position in range(tap_count):
        summed = summed + padded[position:position + length] * kernel[position]
    return jax.nn.silu(summed).astype(jnp.bfloat16)

def ssd_reference(inner_conv, groups_conv, step_size, rates):
    token_count = inner_conv.shape[0]
    span_count = token_count // Q
    per_group = HEADS // G
    heads_x = inner_conv.reshape(span_count, Q, HEADS, P_SIZE)
    groups_bc = groups_conv.reshape(span_count, Q, G, 2, N)
    steps_all = step_size.reshape(span_count, Q, HEADS)
    ahead = jnp.arange(Q)[:, None] >= jnp.arange(Q)[None, :]

    def advance(state, inputs):
        block_x, block_bc, block_dt = inputs
        block_x = block_x.astype(jnp.float32)
        b_group = block_bc[:, :, 0].astype(jnp.float32)
        c_group = block_bc[:, :, 1].astype(jnp.float32)
        b_heads = jnp.repeat(b_group, per_group, axis=1)
        c_heads = jnp.repeat(c_group, per_group, axis=1)
        cum_decay = jnp.cumsum(block_dt * rates, axis=0)
        scores = jnp.einsum('tgn,sgn->gts', c_group, b_group)
        scores = jnp.repeat(scores, per_group, axis=0)
        decay_t = cum_decay.T
        gap = jnp.where(ahead[None], decay_t[:, :, None] - decay_t[:, None, :], -1e+30)
        mixing = (scores * jnp.exp(gap) * block_dt.T[:, None, :]).astype(jnp.bfloat16)
        intra = jnp.einsum('hts,shp->thp', mixing.astype(jnp.float32), block_x)
        inter = jnp.einsum('thn,hnp->thp', c_heads, state, precision=lax.Precision.HIGHEST)
        inter = inter * jnp.exp(cum_decay)[:, :, None]
        span_total = cum_decay[-1]
        weights_in = jnp.exp(span_total[None, :] - cum_decay) * block_dt
        weighted = (b_heads * weights_in[:, :, None]).astype(jnp.bfloat16)
        fresh = jnp.einsum('shn,shp->hnp', weighted.astype(jnp.float32), block_x)
        state = jnp.exp(span_total)[:, None, None] * state + fresh
        return (state, intra + inter)
    start_state = jnp.zeros((HEADS, N, P_SIZE), jnp.float32)
    _, outputs = lax.scan(advance, start_state, (heads_x, groups_bc, steps_all))
    return outputs.reshape(token_count, HEADS * P_SIZE)

def reference(activations, w_inner, w_gate, w_groups, w_step, w_out, conv_inner, conv_groups, step_bias, decay_log, skip_gain, norm_gain):
    inner_in = jnp.dot(activations, w_inner, preferred_element_type=jnp.float32).astype(jnp.bfloat16)
    gate_in = jnp.dot(activations, w_gate, preferred_element_type=jnp.float32).astype(jnp.bfloat16)
    groups_in = jnp.dot(activations, w_groups, preferred_element_type=jnp.float32).astype(jnp.bfloat16)
    step_raw = jnp.dot(activations, w_step, preferred_element_type=jnp.float32)
    inner_conv = causal_conv(inner_in, conv_inner)
    groups_conv = causal_conv(groups_in, conv_groups)
    step_size = jax.nn.softplus(step_raw + step_bias)
    rates = -jnp.exp(decay_log)
    mixed = ssd_reference(inner_conv, groups_conv, step_size, rates)
    mixed = mixed + jnp.repeat(skip_gain, P_SIZE) * inner_conv.astype(jnp.float32)
    gated = mixed * jax.nn.silu(gate_in.astype(jnp.float32))
    mean_square = lax.optimization_barrier(jnp.mean(gated * gated, axis=1, keepdims=True))
    normed = (gated * lax.rsqrt(mean_square + 1e-05) * norm_gain).astype(jnp.bfloat16)
    block_width = INNER // N_HID
    summed = jnp.zeros((activations.shape[0], D), jnp.float32)
    for block in range(N_HID):
        lower = block * block_width
        partial_out = lax.dot_general(normed[:, lower:lower + block_width], w_out[:, lower:lower + block_width], (((1,), (1,)), ((), ())), preferred_element_type=jnp.float32)
        summed = summed + lax.optimization_barrier(partial_out.astype(jnp.bfloat16)).astype(jnp.float32)
    return summed.astype(jnp.bfloat16)
```

```python
import functools

import jax
import jax.numpy as jnp
from jax import lax
from jax.experimental import pallas as pl
from jax.experimental.pallas import tpu as pltpu
from jax.sharding import PartitionSpec as P

HEADS = 64
P_SIZE = 64
N = 128
G = 4
Q = 256
K = 4
INNER = 4096


def from_behind(block, axis, distance):
    devices = range(lax.axis_size(axis))
    route = [(i - distance, i) for i in devices if i - distance in devices]
    return lax.ppermute(block, axis, route)


def carried_in(array, axis, join, neutral):
    place = lax.axis_index(axis)
    gathered = jax.tree.map(
        lambda a, kind: lax.all_gather(a.astype(kind), axis), array, (jnp.bfloat16, jnp.bfloat16)
    )
    state = jax.tree.map(lambda a, e: jnp.zeros_like(a) + jnp.asarray(e, a.dtype), array, neutral)

    def one(step, state):
        return join(
            state,
            jax.tree.map(
                lambda a, own: lax.dynamic_index_in_dim(a, step, 0, False).astype(own.dtype),
                gathered,
                array,
            ),
        )

    return lax.fori_loop(0, place, one, state)


def causal_conv(values, before, kernel):
    length = values.shape[0]
    extended = jnp.concatenate([before, values], axis=0)
    summed = jnp.zeros(values.shape, jnp.float32)
    for position in range(kernel.shape[0]):
        summed = (
            summed + extended[position : position + length].astype(jnp.float32) * kernel[position]
        )
    return jax.nn.silu(summed).astype(jnp.bfloat16)


def combine_states(earlier, later):
    return (earlier[0] * later[0], later[0][:, None, None] * earlier[1] + later[1])


def roll_state(state, inputs):
    total_here, fresh_here = inputs
    return (jnp.exp(total_here)[:, None, None] * state + fresh_here, state)


def local_general(
    activations,
    w_inner,
    w_gate,
    w_groups,
    w_step,
    w_out,
    conv_inner,
    conv_groups,
    step_bias,
    decay_log,
    skip_gain,
    norm_gain,
):
    tok_rows = activations.shape[0]
    heads_dev = step_bias.shape[0]
    width_dev = w_inner.shape[1]
    head_block = lax.axis_index("hid")
    group_cols = 2 * N
    group_index = head_block * heads_dev // (HEADS // G)
    step_cols = lax.dynamic_slice_in_dim(w_step, head_block * heads_dev, heads_dev, 1)
    own_cols = lax.dynamic_slice_in_dim(w_groups, group_index * group_cols, group_cols, 1)
    piece_inner = lax.all_gather(w_inner, "seq", axis=0, tiled=True)
    piece_gate = lax.all_gather(w_gate, "seq", axis=0, tiled=True)
    piece_groups = lax.all_gather(own_cols, "seq", axis=0, tiled=True)
    piece_step = lax.all_gather(step_cols, "seq", axis=0, tiled=True)
    piece_out = lax.all_gather(w_out, "seq", axis=0, tiled=True)
    acc_inner = jnp.dot(activations, piece_inner, preferred_element_type=jnp.float32)
    acc_gate = jnp.dot(activations, piece_gate, preferred_element_type=jnp.float32)
    acc_groups = jnp.dot(activations, piece_groups, preferred_element_type=jnp.float32)
    acc_step = jnp.dot(activations, piece_step, preferred_element_type=jnp.float32)
    groups_in = acc_groups.astype(jnp.bfloat16)
    inner_in = acc_inner.astype(jnp.bfloat16)
    gate_in = acc_gate.astype(jnp.bfloat16)
    own_out_rows = lax.all_to_all(piece_out, "hid", split_axis=0, concat_axis=1, tiled=True)
    conv_group = lax.dynamic_slice_in_dim(conv_groups, group_index * group_cols, group_cols, 1)
    tail_rows = K - 1
    inner_prev, groups_prev = from_behind(
        (inner_in[tok_rows - tail_rows :], groups_in[tok_rows - tail_rows :]), "seq", 1
    )
    inner_conv = causal_conv(inner_in, inner_prev, conv_inner)
    groups_conv = causal_conv(groups_in, groups_prev, conv_group)
    step_size = jax.nn.softplus(acc_step + step_bias)
    rates = -jnp.exp(decay_log)
    span_count = tok_rows // Q
    heads_x = inner_conv.reshape(span_count, Q, heads_dev, P_SIZE)
    b_in = groups_conv[:, :N].reshape(span_count, Q, N)
    c_out = groups_conv[:, N:].reshape(span_count, Q, N)
    block_dt = step_size.reshape(span_count, Q, heads_dev)
    cum_decay = jnp.cumsum(block_dt * rates, axis=1)
    scores = jnp.einsum("ctn,csn->cts", c_out, b_in, preferred_element_type=jnp.float32)
    ahead = jnp.arange(Q)[:, None] >= jnp.arange(Q)[None, :]
    decay_t = jnp.swapaxes(cum_decay, 1, 2)
    gap = jnp.where(ahead, decay_t[:, :, :, None] - decay_t[:, :, None, :], -1e30)
    mixing = (scores[:, None] * jnp.exp(gap) * jnp.swapaxes(block_dt, 1, 2)[:, :, None, :]).astype(
        jnp.bfloat16
    )
    intra = jnp.einsum("chts,cshp->cthp", mixing, heads_x, preferred_element_type=jnp.float32)
    span_total = cum_decay[:, -1]
    weights_in = jnp.exp(span_total[:, None, :] - cum_decay) * block_dt
    weighted = (b_in[:, :, None, :] * weights_in[:, :, :, None]).astype(jnp.bfloat16)
    fresh = jnp.einsum("cshn,cshp->chnp", weighted, heads_x, preferred_element_type=jnp.float32)
    zero_state = jnp.zeros((heads_dev, N, P_SIZE), jnp.float32)
    local_end, starts = lax.scan(roll_state, zero_state, (span_total, fresh))
    log_total = jnp.sum(span_total, axis=0)
    prior = jnp.cumsum(span_total, axis=0) - span_total
    identity = (jnp.ones((heads_dev,), jnp.float32), zero_state)
    state_in = carried_in((jnp.exp(log_total), local_end), "seq", combine_states, identity)[1]
    span_in = starts + jnp.exp(prior)[:, :, None, None] * state_in[None]
    inter = jnp.einsum(
        "ctn,chnp->cthp", c_out.astype(jnp.float32), span_in, precision=lax.Precision.HIGHEST
    )
    inter = inter * jnp.exp(cum_decay)[:, :, :, None]
    mixed = (intra + inter).reshape(tok_rows, width_dev) + jnp.repeat(
        skip_gain, P_SIZE
    ) * inner_conv.astype(jnp.float32)
    gated = mixed * jax.nn.silu(gate_in.astype(jnp.float32))
    squares = lax.psum(jnp.sum(gated * gated, axis=1), "hid")
    normed = (gated * lax.rsqrt(squares / INNER + 1e-05)[:, None] * norm_gain).astype(jnp.bfloat16)
    start_sum = jnp.zeros((tok_rows, own_out_rows.shape[0]), jnp.float32)
    total = start_sum
    piece = lax.all_gather(normed, "hid", axis=1, tiled=True)
    block_count = piece.shape[1] // width_dev
    for block in range(block_count):
        cols = piece[:, block * width_dev : (block + 1) * width_dev]
        weight_cols = lax.dynamic_slice_in_dim(own_out_rows, block * width_dev, width_dev, 1)
        partial_out = lax.dot_general(
            cols, weight_cols, (((1,), (1,)), ((), ())), preferred_element_type=jnp.float32
        )
        total = total + lax.optimization_barrier(partial_out.astype(jnp.bfloat16)).astype(
            jnp.float32
        )
    return total.astype(jnp.bfloat16)


CORES = 2
HALO = 16
LANES = 128


def both_cores(moves):
    return [(CORES * a + c, CORES * b + c) for a, b in moves for c in range(CORES)]


INWARD = both_cores([(0, 1), (3, 2)])
OUTWARD = both_cores([(1, 0), (2, 3)])
MIDDLE = both_cores([(1, 2), (2, 1)])
MIDDLE_UP = both_cores([(1, 2)])
NEAR = INWARD + OUTWARD


def other_core(block):
    return lax.ppermute(block, "seq", [(i, i ^ 1) for i in range(lax.axis_size("seq"))])


def along(block, route):
    return lax.ppermute(block, "seq", route)


def across(block, flip):
    return lax.ppermute(block, "hid", [(i, i ^ flip) for i in range(lax.axis_size("hid"))])


def after(block, *earlier):
    return lax.optimization_barrier((block,) + earlier)[0]


def silu(v):
    return v / (1.0 + jnp.exp(-v))


def convolved(window, taps, rows):
    summed = window[HALO : HALO + rows] * taps[K - 1 : K]
    for position in range(K - 1):
        shifted = pltpu.roll(window, K - 1 - position, 0)
        summed = summed + shifted[HALO : HALO + rows] * taps[position : position + 1]
    return silu(summed).astype(jnp.bfloat16)


def pair_of(low_half, left, right):
    return jnp.where(low_half, left, right)


def scan_kernel(
    inner_ref, groups_ref, step_ref, taps_ref, group_taps_ref, bias_ref, decay_ref, skip_ref,
    y_ref, c_ref, grown_ref, end_ref, total_ref, prior_ref,
):
    span = pl.program_id(0)
    f32, bf16 = jnp.float32, jnp.bfloat16
    exact = lax.Precision.HIGHEST
    half = Q // 2

    @pl.when(span == 0)
    def _():
        end_ref[...] = jnp.zeros_like(end_ref)
        prior_ref[...] = jnp.zeros_like(prior_ref)

    rows = pl.ds(pl.multiple_of(span * Q, Q), Q + HALO)
    groups = convolved(groups_ref[rows, :].astype(f32), group_taps_ref[...], Q)
    b_in, c_out = groups[:, :N], groups[:, N:]
    c_ref[...] = c_out
    scores = lax.dot_general(c_out, b_in, (((1,), (1,)), ((), ())), preferred_element_type=f32)
    t_at = lax.broadcasted_iota(jnp.int32, (Q, Q), 0)
    s_at = lax.broadcasted_iota(jnp.int32, (Q, Q), 1)
    ahead = t_at >= s_at
    scores = jnp.where(ahead, scores, 0.0)
    raw = step_ref[...] + bias_ref[...]
    step = jnp.maximum(raw, 0.0) + jnp.log1p(jnp.exp(-jnp.abs(raw)))
    rated = step * -jnp.exp(decay_ref[...])
    cum = jnp.dot(jnp.where(ahead, 1.0, 0.0), rated, precision=exact, preferred_element_type=f32)
    last = cum[Q - 1 : Q, :]
    prior = prior_ref[...]
    grown_ref[...] = jnp.exp(cum + prior)
    prior_ref[...] = prior + last
    total_ref[...] = prior + last
    cum_t, step_t = cum.T, step.T
    grow = jnp.exp(cum)
    weight = jnp.exp(last - cum) * step
    fade = jnp.exp(last)
    low = lax.broadcasted_iota(jnp.int32, (Q, LANES), 1) < P_SIZE
    per = LANES // P_SIZE
    for j in range(inner_ref.shape[1] // LANES):
        lanes = slice(j * LANES, (j + 1) * LANES)
        x = convolved(inner_ref[rows, lanes].astype(f32), taps_ref[:, lanes], Q)
        x_wide = x.astype(f32)
        parts = []
        for h in (per * j, per * j + 1):
            col = cum[:, h : h + 1]
            row, scale = cum_t[h : h + 1, :], step_t[h : h + 1, :]
            top = scores[:half, :half] * jnp.exp(jnp.minimum(col[:half] - row[:, :half], 0.0)) * scale[:, :half]
            bottom = scores[half:] * jnp.exp(jnp.minimum(col[half:] - row, 0.0)) * scale
            parts.append(
                jnp.concatenate(
                    [
                        jnp.dot(top.astype(bf16), x[:half], preferred_element_type=f32),
                        jnp.dot(bottom.astype(bf16), x, preferred_element_type=f32),
                    ],
                    axis=0,
                )
            )
        y = pair_of(low, parts[0], parts[1])
        a, b = per * j, per * j + 1
        state = end_ref[:, lanes]
        high = state.astype(bf16)
        rest = (state - high.astype(f32)).astype(bf16)
        carried = jnp.dot(c_out, high, preferred_element_type=f32) + jnp.dot(c_out, rest, preferred_element_type=f32)
        y = y + carried * pair_of(low, grow[:, a : a + 1], grow[:, b : b + 1])
        y_ref[:, lanes] = y + x_wide * skip_ref[:, lanes]
        weighted = (x_wide * pair_of(low, weight[:, a : a + 1], weight[:, b : b + 1])).astype(bf16)
        fresh = lax.dot_general(b_in, weighted, (((0,), (0,)), ((), ())), preferred_element_type=f32)
        end_ref[:, lanes] = state * pair_of(low[:1], fade[:, a : a + 1], fade[:, b : b + 1]) + fresh


def scan_segment(inner, groups, step, taps, group_taps, bias, decay, skip):
    tokens, width = step.shape[0], inner.shape[1]
    whole = lambda a: pl.BlockSpec(a.shape, lambda i: (0,) * a.ndim)
    spans = lambda w: pl.BlockSpec((Q, w), lambda i: (i, 0))
    fixed = lambda shape: pl.BlockSpec(shape, lambda i: (0, 0))
    f32 = jnp.float32
    return pl.pallas_call(
        scan_kernel,
        grid=(tokens // Q,),
        in_specs=[whole(inner), whole(groups), spans(LANES)] + [whole(a) for a in (taps, group_taps, bias, decay, skip)],
        out_specs=[spans(width), spans(N), spans(LANES), fixed((N, width)), fixed((1, LANES))],
        out_shape=[
            jax.ShapeDtypeStruct((tokens, width), f32),
            jax.ShapeDtypeStruct((tokens, N), jnp.bfloat16),
            jax.ShapeDtypeStruct((tokens, LANES), f32),
            jax.ShapeDtypeStruct((N, width), f32),
            jax.ShapeDtypeStruct((1, LANES), f32),
        ],
        scratch_shapes=[pltpu.VMEM((1, LANES), f32)],
        compiler_params=pltpu.CompilerParams(vmem_limit_bytes=40 * 1024 * 1024),
        cost_estimate=pl.CostEstimate(flops=tokens * width * 1000, bytes_accessed=tokens * width * 8, transcendentals=tokens * width * 4),
        name="scan_segment",
    )(inner, groups, step, taps, group_taps, bias, decay, skip)


def carry_kernel(y_ref, c_ref, grown_ref, state_ref, out_ref):
    f32, bf16 = jnp.float32, jnp.bfloat16
    low = lax.broadcasted_iota(jnp.int32, (Q, LANES), 1) < P_SIZE
    per = LANES // P_SIZE
    c_out, grown = c_ref[...], grown_ref[...]
    for j in range(y_ref.shape[1] // LANES):
        lanes = slice(j * LANES, (j + 1) * LANES)
        state = state_ref[:, lanes]
        high = state.astype(bf16)
        rest = (state - high.astype(f32)).astype(bf16)
        carried = jnp.dot(c_out, high, preferred_element_type=f32) + jnp.dot(c_out, rest, preferred_element_type=f32)
        a, b = per * j, per * j + 1
        out_ref[:, lanes] = y_ref[:, lanes] + carried * pair_of(low, grown[:, a : a + 1], grown[:, b : b + 1])


def add_carried(y, c_out, grown, state):
    tokens, width = y.shape
    spans = lambda w: pl.BlockSpec((Q, w), lambda i: (i, 0))
    return pl.pallas_call(
        carry_kernel,
        grid=(tokens // Q,),
        in_specs=[spans(width), spans(N), spans(LANES), pl.BlockSpec(state.shape, lambda i: (0, 0))],
        out_specs=spans(width),
        out_shape=jax.ShapeDtypeStruct(y.shape, y.dtype),
        input_output_aliases={0: 0},
        cost_estimate=pl.CostEstimate(flops=tokens * width * N * 4, bytes_accessed=tokens * width * 8, transcendentals=0),
        name="add_carried",
    )(y, c_out, grown, state)


def dot(a, b):
    return jnp.dot(a, b, preferred_element_type=jnp.float32)


def local_paired(
    activations, w_inner, w_gate, w_groups, w_step, w_out, conv_inner, conv_groups, step_bias, decay_log, skip_gain, norm_gain
):
    f32, bf16 = jnp.float32, jnp.bfloat16
    tokens, depth = activations.shape
    heads_dev = step_bias.shape[0]
    width = w_inner.shape[1]
    rows = w_inner.shape[0]
    place, head_block = lax.axis_index("seq"), lax.axis_index("hid")
    plane, core = place // CORES, place % CORES
    lower = plane < 2
    middle = (plane == 1) | (plane == 2)
    group_cols = 2 * N
    group_index = head_block * heads_dev // (HEADS // G)
    pad = LANES - heads_dev

    w_small = jnp.concatenate(
        [
            lax.dynamic_slice_in_dim(w_groups, group_index * group_cols, group_cols, 1),
            jnp.pad(lax.dynamic_slice_in_dim(w_step, head_block * heads_dev, heads_dev, 1), ((0, 0), (0, pad))),
        ],
        axis=1,
    )
    devices = lax.axis_size("seq")
    before = lax.ppermute(activations[tokens - HALO :], "seq", [(i, i + 1) for i in range(devices - 1)])
    own = jnp.concatenate([before, activations], axis=0)
    quarter = depth // lax.axis_size("hid")
    lent = lax.dynamic_slice_in_dim(own, head_block * quarter, quarter, 1)

    small_far = along(w_small, MIDDLE)
    small_out = along(w_small, INWARD)
    lent_here = along(lent, INWARD)
    inner_far = along(after(w_inner, small_far), MIDDLE)
    inner_out = along(after(w_inner, small_out), INWARD)
    small_end = along(after(small_out, small_far), MIDDLE)
    gate_far = along(after(w_gate, inner_far), MIDDLE)
    gate_out = along(after(w_gate, lent_here, inner_out), INWARD)
    inner_end = along(after(inner_out, inner_far), MIDDLE)
    gate_end = along(after(gate_out, inner_end), MIDDLE)
    out_near = along(after(w_out, gate_out), NEAR)
    out_far = along(after(w_out, gate_far, inner_end), MIDDLE)
    out_end = along(after(out_near, gate_end), MIDDLE)
    out_far_on = along(after(out_far, out_near), OUTWARD)
    out_end_on = along(out_end, OUTWARD)

    lent_by = jnp.stack([lent_here] + [across(lent_here, flip) for flip in (1, 2, 3)])

    mirrored = lax.axis_size("hid") - 1 - plane
    partner = plane ^ 1
    planes_of = (plane, mirrored, partner, mirrored ^ 1)

    def mine(plane_at, which):
        start = (plane_at * CORES + which) * rows
        return lax.dynamic_slice_in_dim(own, start, rows, 1)

    def borrowed(plane_at, which):
        block = lax.dynamic_index_in_dim(lent_by, plane_at ^ head_block, 0, False)
        return lax.dynamic_slice_in_dim(block, which * rows, rows, 1)

    def project(pieces, source, skip_rows=0):
        total = None
        for plane_at, (here, there) in zip(planes_of, pieces):
            for block, which in ((here, core), (there, 1 - core)):
                term = dot(source(plane_at, which)[skip_rows:], block)
                total = term if total is None else total + term
        return total

    def with_other(*blocks):
        return [(b, other_core(b)) for b in blocks]

    small = with_other(w_small, small_far, small_out, small_end)
    inner = with_other(w_inner, inner_far, inner_out, inner_end)
    gate = with_other(w_gate, gate_far, gate_out, gate_end)

    group_taps = lax.dynamic_slice_in_dim(conv_groups, group_index * group_cols, group_cols, 1)
    lane_row = lambda v: jnp.pad(v, (0, pad))[None, :]
    consts = (conv_inner, group_taps, lane_row(step_bias), lane_row(decay_log), jnp.repeat(skip_gain, P_SIZE)[None, :])
    results = []
    for source in (mine, borrowed):
        small_in = project(small, source)
        inner_in = project(inner, source).astype(bf16)
        results.append(
            scan_segment(inner_in, small_in[:, :group_cols].astype(bf16), small_in[HALO:, group_cols:], *consts)
        )
    (y_mine, c_mine, grown_mine, end_mine, total_mine), (y_lent, c_lent, grown_lent, end_lent, total_lent) = results

    pick = lambda a, b: jnp.where(lower, a, b)
    ends = jnp.stack([pick(end_lent, end_mine), pick(end_mine, end_lent)]).astype(bf16)
    totals = jnp.stack([pick(total_lent, total_mine), pick(total_mine, total_lent)])
    ends_other, totals_other = other_core(ends), other_core(totals)
    fades = lambda t: jnp.repeat(jnp.exp(t[:, :heads_dev]), P_SIZE, axis=1)
    chain = []
    for which in range(2):
        for c in range(CORES):
            chain.append(
                (
                    fades(jnp.where(core == c, totals[which], totals_other[which])),
                    jnp.where(core == c, ends[which], ends_other[which]).astype(f32),
                )
            )
    run = jnp.zeros_like(end_mine)
    for fade, end in chain:
        run = fade * run + end
    state = along(run.astype(bf16), MIDDLE_UP).astype(f32)
    starts = []
    for fade, end in chain:
        starts.append(state)
        state = fade * state + end
    first = jnp.where(core == 0, starts[0], starts[1])
    second = jnp.where(core == 0, starts[2], starts[3])
    y_mine = add_carried(y_mine, c_mine, grown_mine, pick(second, first))
    y_lent = add_carried(y_lent, c_lent, grown_lent, pick(first, second))

    def gated_of(y, source):
        gate_in = project(gate, source, HALO).astype(bf16).astype(f32)
        gated = y * silu(gate_in)
        return (gated * norm_gain).astype(bf16), jnp.sum(gated * gated, axis=1)

    scaled_lent, squares_lent = gated_of(y_lent, borrowed)
    back, squares_back = along(scaled_lent, OUTWARD), along(squares_lent, OUTWARD)
    scaled_mine, squares_mine = gated_of(y_mine, mine)
    scaled = jnp.where(middle, scaled_mine, back)
    squares = jnp.where(middle, squares_mine, squares_back)
    scaled = jnp.concatenate([scaled, other_core(scaled)], axis=0)
    squares = jnp.concatenate([squares, other_core(squares)], axis=0)
    squares = squares + across(squares, 1)
    squares = squares + across(squares, 2)
    norm = lax.rsqrt(squares / INNER + 1e-05)

    far_first, far_second = jnp.where(middle, out_far, out_far_on), jnp.where(middle, out_end, out_end_on)
    far_index = jnp.where(lower, 2, 1)
    near_low, near_high = pick_two(plane % 2 == 0, w_out, out_near)
    far_low, far_high = pick_two(far_index % 2 == 0, far_first, far_second)

    def partial_of(weight):
        return lax.dot_general(scaled, weight, (((1,), (1,)), ((), ())), preferred_element_type=f32).astype(bf16)

    seqs, hids = lax.axis_size("seq"), lax.axis_size("hid")

    def deliver(low, high, is_near):
        same_pair = (head_block // 2 == plane // 2) == is_near
        kept = jnp.where(head_block % 2 == 0, low, high)
        total = jnp.where(same_pair, kept, jnp.zeros_like(kept)).astype(f32)
        for flip in (1, 2, 3):
            route = [
                (s * hids + h, s * hids + (h ^ flip))
                for s in range(seqs)
                for h in range(hids)
                if (((h ^ flip) // 2) == (s // CORES) // 2) == is_near
            ]
            sent = jnp.where((head_block ^ flip) % 2 == 0, low, high)
            total = total + lax.ppermute(sent, ("seq", "hid"), route).astype(f32)
        return total

    near = deliver(partial_of(near_low), partial_of(near_high), True)
    far = deliver(partial_of(far_low), partial_of(far_high), False)
    features = ((near + far) * norm[:, None]).astype(bf16)
    got = other_core(features[tokens:])
    kept = features[:tokens]
    return jnp.concatenate([jnp.where(core == 0, kept, got), jnp.where(core == 0, got, kept)], axis=1)


def pick_two(swap, a, b):
    return jnp.where(swap, a, b), jnp.where(swap, b, a)


def plan_of(mesh):
    planes = mesh.shape["seq"] // CORES
    return local_paired if planes == 4 and mesh.shape["hid"] == planes else local_general


def solution(mesh):
    in_specs = (
        P("seq", None),
        P("seq", "hid"),
        P("seq", "hid"),
        P("seq", None),
        P("seq", None),
        P("seq", "hid"),
        P(None, "hid"),
        P(),
        P("hid"),
        P("hid"),
        P("hid"),
        P("hid"),
    )
    out_specs = P("seq", "hid")
    return jax.shard_map(plan_of(mesh), mesh=mesh, in_specs=in_specs, out_specs=out_specs, check_vma=False)
```

```python
import functools

import jax
import jax.numpy as jnp
from jax import lax
from jax.experimental import pallas as pl
from jax.experimental.pallas import tpu as pltpu
from jax.sharding import PartitionSpec as P

HEADS = 64
P_SIZE = 64
N = 128
G = 4
Q = 256
K = 4
INNER = 4096


def from_behind(block, axis, distance):
    devices = range(lax.axis_size(axis))
    route = [(i - distance, i) for i in devices if i - distance in devices]
    return lax.ppermute(block, axis, route)


def carried_in(array, axis, join, neutral):
    place = lax.axis_index(axis)
    gathered = jax.tree.map(
        lambda a, kind: lax.all_gather(a.astype(kind), axis), array, (jnp.bfloat16, jnp.bfloat16)
    )
    state = jax.tree.map(lambda a, e: jnp.zeros_like(a) + jnp.asarray(e, a.dtype), array, neutral)

    def one(step, state):
        return join(
            state,
            jax.tree.map(
                lambda a, own: lax.dynamic_index_in_dim(a, step, 0, False).astype(own.dtype),
                gathered,
                array,
            ),
        )

    return lax.fori_loop(0, place, one, state)


def causal_conv(values, before, kernel):
    length = values.shape[0]
    extended = jnp.concatenate([before, values], axis=0)
    summed = jnp.zeros(values.shape, jnp.float32)
    for position in range(kernel.shape[0]):
        summed = (
            summed + extended[position : position + length].astype(jnp.float32) * kernel[position]
        )
    return jax.nn.silu(summed).astype(jnp.bfloat16)


def combine_states(earlier, later):
    return (earlier[0] * later[0], later[0][:, None, None] * earlier[1] + later[1])


def roll_state(state, inputs):
    total_here, fresh_here = inputs
    return (jnp.exp(total_here)[:, None, None] * state + fresh_here, state)


def local_general(
    activations,
    w_inner,
    w_gate,
    w_groups,
    w_step,
    w_out,
    conv_inner,
    conv_groups,
    step_bias,
    decay_log,
    skip_gain,
    norm_gain,
):
    tok_rows = activations.shape[0]
    heads_dev = step_bias.shape[0]
    width_dev = w_inner.shape[1]
    head_block = lax.axis_index("hid")
    group_cols = 2 * N
    group_index = head_block * heads_dev // (HEADS // G)
    step_cols = lax.dynamic_slice_in_dim(w_step, head_block * heads_dev, heads_dev, 1)
    own_cols = lax.dynamic_slice_in_dim(w_groups, group_index * group_cols, group_cols, 1)
    piece_inner = lax.all_gather(w_inner, "seq", axis=0, tiled=True)
    piece_gate = lax.all_gather(w_gate, "seq", axis=0, tiled=True)
    piece_groups = lax.all_gather(own_cols, "seq", axis=0, tiled=True)
    piece_step = lax.all_gather(step_cols, "seq", axis=0, tiled=True)
    piece_out = lax.all_gather(w_out, "seq", axis=0, tiled=True)
    acc_inner = jnp.dot(activations, piece_inner, preferred_element_type=jnp.float32)
    acc_gate = jnp.dot(activations, piece_gate, preferred_element_type=jnp.float32)
    acc_groups = jnp.dot(activations, piece_groups, preferred_element_type=jnp.float32)
    acc_step = jnp.dot(activations, piece_step, preferred_element_type=jnp.float32)
    groups_in = acc_groups.astype(jnp.bfloat16)
    inner_in = acc_inner.astype(jnp.bfloat16)
    gate_in = acc_gate.astype(jnp.bfloat16)
    own_out_rows = lax.all_to_all(piece_out, "hid", split_axis=0, concat_axis=1, tiled=True)
    conv_group = lax.dynamic_slice_in_dim(conv_groups, group_index * group_cols, group_cols, 1)
    tail_rows = K - 1
    inner_prev, groups_prev = from_behind(
        (inner_in[tok_rows - tail_rows :], groups_in[tok_rows - tail_rows :]), "seq", 1
    )
    inner_conv = causal_conv(inner_in, inner_prev, conv_inner)
    groups_conv = causal_conv(groups_in, groups_prev, conv_group)
    step_size = jax.nn.softplus(acc_step + step_bias)
    rates = -jnp.exp(decay_log)
    span_count = tok_rows // Q
    heads_x = inner_conv.reshape(span_count, Q, heads_dev, P_SIZE)
    b_in = groups_conv[:, :N].reshape(span_count, Q, N)
    c_out = groups_conv[:, N:].reshape(span_count, Q, N)
    block_dt = step_size.reshape(span_count, Q, heads_dev)
    cum_decay = jnp.cumsum(block_dt * rates, axis=1)
    scores = jnp.einsum("ctn,csn->cts", c_out, b_in, preferred_element_type=jnp.float32)
    ahead = jnp.arange(Q)[:, None] >= jnp.arange(Q)[None, :]
    decay_t = jnp.swapaxes(cum_decay, 1, 2)
    gap = jnp.where(ahead, decay_t[:, :, :, None] - decay_t[:, :, None, :], -1e30)
    mixing = (scores[:, None] * jnp.exp(gap) * jnp.swapaxes(block_dt, 1, 2)[:, :, None, :]).astype(
        jnp.bfloat16
    )
    intra = jnp.einsum("chts,cshp->cthp", mixing, heads_x, preferred_element_type=jnp.float32)
    span_total = cum_decay[:, -1]
    weights_in = jnp.exp(span_total[:, None, :] - cum_decay) * block_dt
    weighted = (b_in[:, :, None, :] * weights_in[:, :, :, None]).astype(jnp.bfloat16)
    fresh = jnp.einsum("cshn,cshp->chnp", weighted, heads_x, preferred_element_type=jnp.float32)
    zero_state = jnp.zeros((heads_dev, N, P_SIZE), jnp.float32)
    local_end, starts = lax.scan(roll_state, zero_state, (span_total, fresh))
    log_total = jnp.sum(span_total, axis=0)
    prior = jnp.cumsum(span_total, axis=0) - span_total
    identity = (jnp.ones((heads_dev,), jnp.float32), zero_state)
    state_in = carried_in((jnp.exp(log_total), local_end), "seq", combine_states, identity)[1]
    span_in = starts + jnp.exp(prior)[:, :, None, None] * state_in[None]
    inter = jnp.einsum(
        "ctn,chnp->cthp", c_out.astype(jnp.float32), span_in, precision=lax.Precision.HIGHEST
    )
    inter = inter * jnp.exp(cum_decay)[:, :, :, None]
    mixed = (intra + inter).reshape(tok_rows, width_dev) + jnp.repeat(
        skip_gain, P_SIZE
    ) * inner_conv.astype(jnp.float32)
    gated = mixed * jax.nn.silu(gate_in.astype(jnp.float32))
    squares = lax.psum(jnp.sum(gated * gated, axis=1), "hid")
    normed = (gated * lax.rsqrt(squares / INNER + 1e-05)[:, None] * norm_gain).astype(jnp.bfloat16)
    start_sum = jnp.zeros((tok_rows, own_out_rows.shape[0]), jnp.float32)
    total = start_sum
    piece = lax.all_gather(normed, "hid", axis=1, tiled=True)
    block_count = piece.shape[1] // width_dev
    for block in range(block_count):
        cols = piece[:, block * width_dev : (block + 1) * width_dev]
        weight_cols = lax.dynamic_slice_in_dim(own_out_rows, block * width_dev, width_dev, 1)
        partial_out = lax.dot_general(
            cols, weight_cols, (((1,), (1,)), ((), ())), preferred_element_type=jnp.float32
        )
        total = total + lax.optimization_barrier(partial_out.astype(jnp.bfloat16)).astype(
            jnp.float32
        )
    return total.astype(jnp.bfloat16)


CORES = 2
HALO = 16
LANES = 128
VMEM = 28 * 1024 * 1024
COST = pl.CostEstimate(flops=1, bytes_accessed=1, transcendentals=0)


def both_cores(moves):
    return [(CORES * a + c, CORES * b + c) for a, b in moves for c in range(CORES)]


INWARD = both_cores([(0, 1), (3, 2)])
OUTWARD = both_cores([(1, 0), (2, 3)])
MIDDLE = both_cores([(1, 2), (2, 1)])
MIDDLE_UP = both_cores([(1, 2)])
NEAR = INWARD + OUTWARD


def other_core(block):
    return lax.ppermute(block, "seq", [(i, i ^ 1) for i in range(lax.axis_size("seq"))])


def along(block, route):
    return lax.ppermute(block, "seq", route)


def across(block, flip):
    return lax.ppermute(block, "hid", [(i, i ^ flip) for i in range(lax.axis_size("hid"))])


def silu(v):
    return v / (1.0 + jnp.exp(-v))


def convolved(window, taps, rows):
    summed = window[HALO : HALO + rows] * taps[K - 1 : K]
    for position in range(K - 1):
        shifted = pltpu.roll(window, K - 1 - position, 0)
        summed = summed + shifted[HALO : HALO + rows] * taps[position : position + 1]
    return silu(summed).astype(jnp.bfloat16)


def pair_of(low_half, left, right):
    return jnp.where(low_half, left, right)


def scan_kernel(
    first_ref, step_ref, taps_ref, group_taps_ref, bias_ref, decay_ref, skip_ref,
    y_ref, c_ref, grown_ref, end_ref, through_ref, prior_ref,
):
    span = pl.program_id(0)
    f32, bf16 = jnp.float32, jnp.bfloat16
    exact = lax.Precision.HIGHEST
    half = Q // 2

    @pl.when(span == 0)
    def _():
        end_ref[...] = jnp.zeros_like(end_ref)
        prior_ref[...] = jnp.zeros_like(prior_ref)

    width = y_ref.shape[1]
    rows = pl.ds(pl.multiple_of(span * Q, Q), Q + HALO)
    rounded = lambda columns: first_ref[rows, columns].astype(f32)
    groups = convolved(rounded(slice(width, width + 2 * N)), group_taps_ref[...], Q)
    b_in, c_out = groups[:, :N], groups[:, N:]
    c_ref[...] = c_out
    scores = lax.dot_general(c_out, b_in, (((1,), (1,)), ((), ())), preferred_element_type=f32)
    t_at = lax.broadcasted_iota(jnp.int32, (Q, Q), 0)
    s_at = lax.broadcasted_iota(jnp.int32, (Q, Q), 1)
    ahead = t_at >= s_at
    scores = jnp.where(ahead, scores, 0.0)
    raw = step_ref[...] + bias_ref[...]
    step = jnp.maximum(raw, 0.0) + jnp.log1p(jnp.exp(-jnp.abs(raw)))
    rated = step * -jnp.exp(decay_ref[...])
    cum = jnp.dot(jnp.where(ahead, 1.0, 0.0), rated, precision=exact, preferred_element_type=f32)
    last = cum[Q - 1 : Q, :]
    prior = prior_ref[...]
    grown_ref[...] = jnp.exp(cum + prior)
    prior_ref[...] = prior + last
    through = jnp.exp(prior + last)
    cum_t, step_t = cum.T, step.T
    grow = jnp.exp(cum)
    weight = jnp.exp(last - cum) * step
    fade = jnp.exp(last)
    low = lax.broadcasted_iota(jnp.int32, (Q, LANES), 1) < P_SIZE
    per = LANES // P_SIZE
    for j in range(width // LANES):
        lanes = slice(j * LANES, (j + 1) * LANES)
        x = convolved(rounded(lanes), taps_ref[:, lanes], Q)
        x_wide = x.astype(f32)
        parts = []
        for h in (per * j, per * j + 1):
            col = cum[:, h : h + 1]
            row, scale = cum_t[h : h + 1, :], step_t[h : h + 1, :]
            top = scores[:half, :half] * jnp.exp(jnp.minimum(col[:half] - row[:, :half], 0.0)) * scale[:, :half]
            bottom = scores[half:] * jnp.exp(jnp.minimum(col[half:] - row, 0.0)) * scale
            parts.append(
                jnp.concatenate(
                    [
                        jnp.dot(top.astype(bf16), x[:half], preferred_element_type=f32),
                        jnp.dot(bottom.astype(bf16), x, preferred_element_type=f32),
                    ],
                    axis=0,
                )
            )
        y = pair_of(low, parts[0], parts[1])
        a, b = per * j, per * j + 1
        state = end_ref[:, lanes]
        high = state.astype(bf16)
        rest = (state - high.astype(f32)).astype(bf16)
        carried = jnp.dot(c_out, high, preferred_element_type=f32) + jnp.dot(c_out, rest, preferred_element_type=f32)
        y = y + carried * pair_of(low, grow[:, a : a + 1], grow[:, b : b + 1])
        y_ref[:, lanes] = y + x_wide * skip_ref[:, lanes]
        weighted = (x_wide * pair_of(low, weight[:, a : a + 1], weight[:, b : b + 1])).astype(bf16)
        fresh = lax.dot_general(b_in, weighted, (((0,), (0,)), ((), ())), preferred_element_type=f32)
        end_ref[:, lanes] = state * pair_of(low[:1], fade[:, a : a + 1], fade[:, b : b + 1]) + fresh
        through_ref[:, lanes] = pair_of(low[:1], through[:, a : a + 1], through[:, b : b + 1])


def scan_segment(first, step, taps, group_taps, bias, decay, skip):
    tokens, width = step.shape[0], taps.shape[1]
    whole = lambda a: pl.BlockSpec(a.shape, lambda i: (0,) * a.ndim)
    spans = lambda w: pl.BlockSpec((Q, w), lambda i: (i, 0))
    fixed = lambda shape: pl.BlockSpec(shape, lambda i: (0, 0))
    f32 = jnp.float32
    return pl.pallas_call(
        scan_kernel,
        grid=(tokens // Q,),
        in_specs=[whole(first), spans(LANES)] + [whole(a) for a in (taps, group_taps, bias, decay, skip)],
        out_specs=[spans(width), spans(N), spans(LANES), fixed((N, width)), fixed((1, width))],
        out_shape=[
            jax.ShapeDtypeStruct((tokens, width), f32),
            jax.ShapeDtypeStruct((tokens, N), jnp.bfloat16),
            jax.ShapeDtypeStruct((tokens, LANES), f32),
            jax.ShapeDtypeStruct((N, width), f32),
            jax.ShapeDtypeStruct((1, width), f32),
        ],
        scratch_shapes=[pltpu.VMEM((1, LANES), f32)],
        compiler_params=pltpu.CompilerParams(vmem_limit_bytes=VMEM),
        cost_estimate=COST,
        name="scan_segment",
    )(first, step, taps, group_taps, bias, decay, skip)


def fetch(at_ref, sources, pieces, source_buf, piece_buf, sems):
    rows = piece_buf.shape[1]
    each = source_buf.shape[1] // len(sources)
    waits = []
    for piece in pieces:
        for part in range(piece.shape[0] // rows):
            i = len(waits)
            columns = pl.ds(pl.multiple_of(at_ref[i] * rows, rows), rows)
            copies = [pltpu.make_async_copy(piece.at[pl.ds(part * rows, rows)], piece_buf.at[i], sems.at[i, 0])]
            for k, source in enumerate(sources):
                first = source.shape[0] - each
                copies.append(
                    pltpu.make_async_copy(
                        source.at[pl.ds(first, each), columns], source_buf.at[i, pl.ds(k * each, each)], sems.at[i, 1 + k]
                    )
                )
            for copy in copies:
                copy.start()
            waits.append(lambda copies=copies: [copy.wait() for copy in copies])
    return waits


def blocks_of(width):
    step = 2 * LANES
    return [slice(n, min(n + step, width)) for n in range(0, width, step)]


def project_kernel(n_sources, count, begun, final, at_ref, *refs):
    sources, pieces, refs = refs[:n_sources], refs[n_sources : n_sources + count], refs[n_sources + count :]
    partial_ref, refs = (refs[0], refs[1:]) if begun else (None, refs)
    outs, (total_ref, source_buf, piece_buf, sems) = refs[:-4], refs[-4:]
    waits = fetch(at_ref, sources, pieces, source_buf, piece_buf, sems)
    for i in range(0, len(waits), 2):
        waits[i]()
        waits[i + 1]()
        for columns in blocks_of(total_ref.shape[1]):
            term = jnp.dot(source_buf[i], piece_buf[i, :, columns], preferred_element_type=jnp.float32)
            term = term + jnp.dot(source_buf[i + 1], piece_buf[i + 1, :, columns], preferred_element_type=jnp.float32)
            if i or begun:
                term = term + (total_ref if i else partial_ref)[:, columns]
            total_ref[:, columns] = term
    if final:
        outs[0][...] = total_ref[:, : outs[0].shape[1]].astype(outs[0].dtype)
        outs[1][...] = total_ref[HALO:, outs[0].shape[1] :]


def project(sources, tokens, pieces, places, partial=None, final=False):
    steps, width = places.shape[0], pieces[0].shape[1]
    rows, height = sum(piece.shape[0] for piece in pieces) // steps, tokens * len(sources)
    f32 = jnp.float32
    if final:
        out_shape = [
            jax.ShapeDtypeStruct((height, width - LANES), jnp.bfloat16),
            jax.ShapeDtypeStruct((height - HALO, LANES), f32),
        ]
    else:
        out_shape = jax.ShapeDtypeStruct((height, width), f32)
    total = [pltpu.VMEM((height, width), f32)] if final else []
    kernel = functools.partial(project_kernel, len(sources), len(pieces), partial is not None, final)

    def body(*refs):
        if final:
            kernel(*refs)
        else:
            kernel(*refs[:-4], *refs[-4:])

    vmem = pl.BlockSpec(memory_space=pltpu.VMEM)
    return pl.pallas_call(
        body,
        in_specs=[pl.BlockSpec(memory_space=pltpu.SMEM)]
        + [pl.BlockSpec(memory_space=pl.ANY)] * (len(sources) + len(pieces))
        + ([vmem] if partial is not None else []),
        out_specs=[vmem] * 2 if final else vmem,
        out_shape=out_shape,
        scratch_shapes=total
        + [
            pltpu.VMEM((steps, height, rows), jnp.bfloat16),
            pltpu.VMEM((steps, rows, width), jnp.bfloat16),
            pltpu.SemaphoreType.DMA((steps, 1 + len(sources))),
        ],
        compiler_params=pltpu.CompilerParams(vmem_limit_bytes=VMEM),
        cost_estimate=COST,
        name="project",
    )(places, *sources, *pieces, *([partial] if partial is not None else []))


def two_rows(row, height):
    high = row.astype(jnp.bfloat16).astype(jnp.float32)
    at = lax.broadcasted_iota(jnp.int32, (height, row.shape[1]), 0)
    return jnp.where(at == 0, high, jnp.where(at == 1, row - high, 0.0)).astype(jnp.bfloat16)


def gate_kernel(count, at_ref, source_ref, *refs):
    pieces, refs = refs[:count], refs[count:]
    begun_ref, y_ref, c_ref, grown_ref, state_ref, gain_ref, *outs, source_buf, piece_buf, sems = refs
    f32, bf16 = jnp.float32, jnp.bfloat16
    waits = fetch(at_ref, [source_ref], pieces, source_buf, piece_buf, sems)
    c_out, grown = c_ref[...], grown_ref[...]
    grown_high = grown.astype(bf16)
    grown_rest = (grown - grown_high.astype(f32)).astype(bf16)
    squares = None
    share = y_ref.shape[0] // len(outs)
    for n, columns in enumerate(blocks_of(y_ref.shape[1])):
        block = columns.stop - columns.start
        total = begun_ref[:, columns]
        for i in range(len(waits)):
            if n == 0:
                waits[i]()
            total = total + jnp.dot(source_buf[i], piece_buf[i, :, columns], preferred_element_type=f32)
        lane = lax.broadcasted_iota(jnp.int32, (LANES, block), 1) + columns.start
        of_head = jnp.where(lane // P_SIZE == lax.broadcasted_iota(jnp.int32, (LANES, block), 0), 1.0, 0.0).astype(bf16)
        spread = jnp.dot(grown_high, of_head, preferred_element_type=f32)
        spread = spread + jnp.dot(grown_rest, of_head, preferred_element_type=f32)
        state = state_ref[:, columns]
        high = state.astype(bf16)
        rest = (state - high.astype(f32)).astype(bf16)
        carried = jnp.dot(c_out, high, preferred_element_type=f32) + jnp.dot(c_out, rest, preferred_element_type=f32)
        gated = (y_ref[:, columns] + carried * spread) * silu(total.astype(bf16).astype(f32))
        scaled = (gated * gain_ref[:, columns]).astype(bf16)
        for k, out in enumerate(outs):
            out[:share, columns] = scaled[k * share : (k + 1) * share]
        square = gated * gated
        for k in range(block // LANES):
            part = square[:, k * LANES : (k + 1) * LANES]
            squares = part if squares is None else squares + part
    ones = jnp.ones((8, LANES), f32)
    for k, out in enumerate(outs):
        part = squares[k * share : (k + 1) * share]
        row = lax.dot_general(
            ones, part, (((1,), (1,)), ((), ())), precision=lax.Precision.HIGHEST, preferred_element_type=f32
        )[:1]
        row = jnp.concatenate([row, jnp.zeros((1, out.shape[1] - share), f32)], axis=1)
        out[share:] = two_rows(row, out.shape[0] - share)


def gate_with(source, pieces, places, begun, part, scanned, state, gain, parts):
    y, c_out, grown = scanned
    tokens, width = y.shape
    steps = places.shape[0]
    rows = sum(piece.shape[0] for piece in pieces) // steps
    vmem = pl.BlockSpec(memory_space=pltpu.VMEM)
    return pl.pallas_call(
        functools.partial(gate_kernel, len(pieces)),
        grid=(1,),
        in_specs=[pl.BlockSpec(memory_space=pltpu.SMEM)]
        + [pl.BlockSpec(memory_space=pl.ANY)] * (1 + len(pieces))
        + [pl.BlockSpec((tokens, width), lambda i: (part, 0))]
        + [vmem] * 5,
        out_specs=[vmem] * parts,
        out_shape=[jax.ShapeDtypeStruct((tokens // parts + HALO, width), jnp.bfloat16)] * parts,
        scratch_shapes=[
            pltpu.VMEM((steps, tokens, rows), jnp.bfloat16),
            pltpu.VMEM((steps, rows, width), jnp.bfloat16),
            pltpu.SemaphoreType.DMA((steps, 2)),
        ],
        compiler_params=pltpu.CompilerParams(vmem_limit_bytes=VMEM),
        cost_estimate=COST,
        name="gate",
    )(places, source, *pieces, begun, y, c_out, grown, state, gain[None, :])


def output_kernel(at_ref, here_ref, back_ref, *refs):
    weights, outs, (block_buf, weight_buf, sems) = refs[:4], refs[4:-3], refs[-3:]
    features = weight_buf.shape[1]
    tokens = block_buf.shape[0] - HALO
    here = pltpu.make_async_copy(here_ref, block_buf, sems.at[2 * len(outs)])
    back = pltpu.make_async_copy(back_ref, block_buf, sems.at[2 * len(outs)])
    stays = at_ref[len(outs)] == 1
    pl.when(stays)(here.start)
    pl.when(jnp.logical_not(stays))(back.start)
    waits = []
    for j in range(len(outs)):
        for i in range(2):
            slot = 2 * j + i
            index, is_near = at_ref[j] % 2, at_ref[j] < 2
            near, far = [pltpu.make_async_copy(weights[k + i].at[index], weight_buf.at[slot], sems.at[slot]) for k in (0, 2)]
            pl.when(is_near)(near.start)
            pl.when(jnp.logical_not(is_near))(far.start)
            waits.append((is_near, near, far))
    pl.when(stays)(here.wait)
    pl.when(jnp.logical_not(stays))(back.wait)
    for j, out in enumerate(outs):
        out[tokens:] = block_buf[tokens:]
        for i in range(2):
            is_near, near, far = waits[2 * j + i]
            pl.when(is_near)(near.wait)
            pl.when(jnp.logical_not(is_near))(far.wait)
            product = lax.dot_general(
                block_buf[:tokens], weight_buf[2 * j + i], (((1,), (1,)), ((), ())), preferred_element_type=jnp.float32
            )
            out[:tokens, i * features : (i + 1) * features] = product.astype(out.dtype)


def output_parts(here, back, pairs, at):
    height, width = here.shape
    features, count = pairs[0].shape[1], at.shape[0] - 1
    vmem, anywhere = pl.BlockSpec(memory_space=pltpu.VMEM), pl.BlockSpec(memory_space=pl.ANY)
    return pl.pallas_call(
        output_kernel,
        in_specs=[pl.BlockSpec(memory_space=pltpu.SMEM)] + [anywhere] * 6,
        out_specs=[vmem] * count,
        out_shape=[jax.ShapeDtypeStruct((height, 2 * features), jnp.bfloat16)] * count,
        scratch_shapes=[
            pltpu.VMEM((height, width), jnp.bfloat16),
            pltpu.VMEM((2 * count, features, width), jnp.bfloat16),
            pltpu.SemaphoreType.DMA((2 * count + 1,)),
        ],
        compiler_params=pltpu.CompilerParams(vmem_limit_bytes=VMEM),
        cost_estimate=COST,
        name="output_parts",
    )(at, here, back, *pairs)


def pack_kernel(at_ref, mine_ref, lent_ref, mine_fade_ref, lent_fade_ref, out_ref):
    lent_first = at_ref[at_ref.shape[0] - 1] == 1
    for which in range(2):
        pick = lent_first if which == 0 else jnp.logical_not(lent_first)
        out_ref[which, :N] = jnp.where(pick, lent_ref[...], mine_ref[...]).astype(out_ref.dtype)
        out_ref[which, N:] = two_rows(jnp.where(pick, lent_fade_ref[...], mine_fade_ref[...]), out_ref.shape[1] - N)


def segments_of(at_ref, own_ref, other_ref):
    core = at_ref[at_ref.shape[0] - 2]
    for which in range(2):
        for c in range(CORES):
            read = lambda rows: jnp.where(
                core == c, own_ref[which, rows].astype(jnp.float32), other_ref[which, rows].astype(jnp.float32)
            )
            fade = read(slice(N, N + HALO))
            yield which, c, fade[:1] + fade[1:2], read(slice(0, N))


def through_kernel(at_ref, own_ref, other_ref, out_ref):
    state = None
    for _, _, fade, end in segments_of(at_ref, own_ref, other_ref):
        state = end if state is None else fade * state + end
    out_ref[...] = state.astype(out_ref.dtype)


def starts_kernel(at_ref, own_ref, other_ref, before_ref, mine_ref, lent_ref):
    lent_first, core = at_ref[at_ref.shape[0] - 1] == 1, at_ref[at_ref.shape[0] - 2]
    state = before_ref[...].astype(jnp.float32)
    for which, c, fade, end in segments_of(at_ref, own_ref, other_ref):
        to_lent = lent_first if which == 0 else jnp.logical_not(lent_first)

        @pl.when((core == c) & to_lent)
        def _(state=state):
            lent_ref[...] = state

        @pl.when((core == c) & jnp.logical_not(to_lent))
        def _(state=state):
            mine_ref[...] = state

        state = fade * state + end


def on_states(kernel, shapes, at, *arrays):
    vmem = pl.BlockSpec(memory_space=pltpu.VMEM)
    return pl.pallas_call(
        kernel,
        in_specs=[pl.BlockSpec(memory_space=pltpu.SMEM)] + [vmem] * len(arrays),
        out_specs=[vmem] * len(shapes),
        out_shape=shapes,
        compiler_params=pltpu.CompilerParams(vmem_limit_bytes=VMEM),
        cost_estimate=COST,
        name="states",
    )(at, *arrays)


def arrange_kernel(moves, count, at_ref, *refs):
    sources, outs, sems = refs[:count], refs[count:-1], refs[-1]
    copies = []
    for k, (source, rows, out, place, condition) in enumerate(moves):
        copy = pltpu.make_async_copy(sources[source].at[rows], outs[out].at[place(at_ref)], sems.at[k])
        copies.append((copy, condition))
    for copy, condition in copies:
        copy.start() if condition is None else pl.when(condition(at_ref))(copy.start)
    for copy, condition in copies:
        copy.wait() if condition is None else pl.when(condition(at_ref))(copy.wait)


def arrange(sources, shapes, moves, at):
    anywhere = pl.BlockSpec(memory_space=pl.ANY)
    return pl.pallas_call(
        functools.partial(arrange_kernel, moves, len(sources)),
        in_specs=[pl.BlockSpec(memory_space=pltpu.SMEM)] + [anywhere] * len(sources),
        out_specs=[pl.BlockSpec(memory_space=pltpu.VMEM)] * len(shapes),
        out_shape=[jax.ShapeDtypeStruct(shape, sources[0].dtype) for shape in shapes],
        scratch_shapes=[pltpu.SemaphoreType.DMA((len(moves),))],
        compiler_params=pltpu.CompilerParams(vmem_limit_bytes=VMEM),
        cost_estimate=COST,
        name="arrange",
    )(at, *sources)


def stacked(blocks, at):
    moves, first = [], 0
    for k, block in enumerate(blocks):
        rows = slice(first, first + block.shape[0])
        moves.append((k, slice(None), 0, lambda at_ref, rows=rows: rows, None))
        first = rows.stop
    return arrange(blocks, [(first,) + blocks[0].shape[1:]], moves, at)[0]


class Order:
    def __init__(self, token):
        self.token = token

    def wait(self, *blocks):
        self.token, *blocks = lax.optimization_barrier((self.token, *blocks))
        return blocks[0] if len(blocks) == 1 else blocks

    def now(self, block):
        return lax.optimization_barrier((block, self.token))[0]


def local_paired(
    activations, w_inner, w_gate, w_groups, w_step, w_out, conv_inner, conv_groups, step_bias, decay_log, skip_gain, norm_gain
):
    f32, bf16 = jnp.float32, jnp.bfloat16
    tokens, depth = activations.shape
    heads_dev = step_bias.shape[0]
    width = w_inner.shape[1]
    place, head_block = lax.axis_index("seq"), lax.axis_index("hid")
    plane, core = place // CORES, place % CORES
    lower = plane < 2
    middle = (plane == 1) | (plane == 2)
    group_cols = 2 * N
    group_index = head_block * heads_dev // (HEADS // G)
    pad = LANES - heads_dev
    devices, chips = lax.axis_size("seq"), lax.axis_size("hid")
    half = tokens // 2
    order = Order(step_bias)
    now, wait = order.now, order.wait

    w_first = jnp.concatenate(
        [
            w_inner,
            lax.dynamic_slice_in_dim(w_groups, group_index * group_cols, group_cols, 1),
            jnp.pad(lax.dynamic_slice_in_dim(w_step, head_block * heads_dev, heads_dev, 1), ((0, 0), (0, pad))),
        ],
        axis=1,
    )
    quarter = depth // chips

    mirrored = chips - 1 - plane
    partner = plane ^ 1
    places_of = lambda *planes: jnp.stack([jnp.clip(p, 0, chips - 1) * CORES + c for p in planes for c in (core, 1 - core)])
    early, late = places_of(plane, mirrored), places_of(partner, mirrored ^ 1)
    group_taps = lax.dynamic_slice_in_dim(conv_groups, group_index * group_cols, group_cols, 1)
    lane_row = lambda v: jnp.pad(v, (0, pad))[None, :]
    consts = (conv_inner, group_taps, lane_row(step_bias), lane_row(decay_log), jnp.repeat(skip_gain, P_SIZE)[None, :])
    rows = w_out.shape[0]
    to = jnp.stack([head_block ^ flip for flip in range(chips)] + [middle.astype(jnp.int32), core, lower.astype(jnp.int32)])
    halo = wait(lax.ppermute(activations[tokens - HALO :], "seq", [(i, i + 1) for i in range(devices - 1)]))
    first_out, first_far = along(now(w_first), INWARD), along(now(w_first), MIDDLE)
    first_x, gate_x = wait(other_core(now(w_first)), other_core(now(w_gate)))
    mine = stacked([halo, activations], now(to))
    lent_out = wait(stacked([lax.dynamic_slice_in_dim(mine, head_block * quarter, quarter, 1), w_out], now(to)))
    near = along(now(lent_out), NEAR)
    first_far, first_out = wait(first_far, first_out)
    first_end = along(now(first_out), MIDDLE)
    far_x, out_x = wait(other_core(now(first_far)), other_core(now(first_out)))
    first_early = [w_first, first_x, first_far, far_x]
    begun_mine = wait(project([mine], tokens + HALO, first_early, now(early)))
    first_end = wait(first_end)
    gate_far = along(now(w_gate), MIDDLE)
    end_x = wait(other_core(now(first_end)))
    first_late = [first_out, out_x, first_end, end_x]
    first_mine, step_mine, near = wait(*project([mine], tokens + HALO, first_late, now(late), begun_mine, True), near)
    lent_rows = HALO + tokens
    lent_here, out_both = wait(
        *arrange(
            [near, w_out],
            [(lent_rows, quarter), (2 * rows, width)],
            [
                (0, slice(0, lent_rows), 0, lambda at: slice(None), None),
                (1, slice(None), 1, lambda at: slice(0, rows), None),
                (0, slice(lent_rows, lent_rows + rows), 1, lambda at: slice(rows, 2 * rows), None),
            ],
            now(to),
        )
    )
    lent_x, lent_y = across(now(lent_here), 1), across(now(lent_here), 2)
    out_two = along(now(out_both), MIDDLE)
    *scanned_mine, gate_far = wait(*scan_segment(now(first_mine), step_mine, *consts), gate_far)
    scanned_mine, end_mine, through_mine = split_scan(scanned_mine)
    gate_out = along(now(w_gate), INWARD)
    lent_x, lent_y = wait(lent_x, lent_y)
    cut = lent_rows // 2 // HALO * HALO
    by_x, by_y = wait(
        *arrange(
            [lent_y, lent_x],
            [(cut, quarter), (lent_rows - cut, quarter)],
            [
                (0, slice(0, cut), 0, lambda at: slice(None), None),
                (1, slice(cut, lent_rows), 1, lambda at: slice(None), None),
            ],
            now(to),
        )
    )
    by_x, by_y = wait(across(now(by_x), 1), across(now(by_y), 2))
    columns = lambda flip, rows=slice(None): lambda at: (rows, pl.ds(at[flip] * quarter, quarter))
    (borrowed,) = arrange(
        [lent_here, lent_x, lent_y, by_x, by_y],
        [(lent_rows, depth)],
        [(flip, slice(None), 0, columns(flip), None) for flip in range(3)]
        + [(3, slice(None), 0, columns(3, slice(0, cut)), None), (4, slice(None), 0, columns(3, slice(cut, lent_rows)), None)],
        now(to),
    )
    borrowed, out_two, gate_out = wait(borrowed, out_two, gate_out)
    out_two_on, gate_end = along(now(out_two), OUTWARD), along(now(gate_out), MIDDLE)
    gate_out_x, gate_far_x = other_core(now(gate_out)), other_core(now(gate_far))
    first_lent, step_lent = wait(
        *project([borrowed], lent_rows, first_early + first_late, now(jnp.concatenate([early, late])), None, True)
    )
    *scanned_lent, gate_end, gate_out_x, gate_far_x = wait(
        *scan_segment(now(first_lent), step_lent, *consts), gate_end, gate_out_x, gate_far_x
    )
    scanned_lent, end_lent, through_lent = split_scan(scanned_lent)

    state = jax.ShapeDtypeStruct((N, width), f32)
    (ends,) = on_states(
        pack_kernel, [jax.ShapeDtypeStruct((2, N + HALO, width), bf16)], now(to), end_mine, end_lent, through_mine, through_lent
    )
    ends = wait(ends)
    ends_other = wait(other_core(now(ends)))
    (run,) = wait(on_states(through_kernel, [jax.ShapeDtypeStruct((N, width), bf16)], now(to), ends, ends_other))
    state_in, gate_end_x = along(now(run), MIDDLE_UP), other_core(now(gate_end))
    gate_early = [w_gate, gate_x, gate_out, gate_out_x, gate_far, gate_far_x]
    gate_begun = wait(project([borrowed, mine], tokens, gate_early, now(places_of(plane, partner, mirrored))))
    state_in, gate_end_x, out_two_on = wait(state_in, gate_end_x, out_two_on)
    everything = lambda at: slice(None)
    (far,) = arrange(
        [out_two, out_two_on],
        [(2 * rows, width)],
        [(0, slice(None), 0, everything, lambda at: at[chips] == 1), (1, slice(None), 0, everything, lambda at: at[chips] == 0)],
        now(to),
    )
    far = wait(far)
    far_x, both_x = other_core(now(far)), other_core(now(out_both))
    state_mine, state_lent = wait(*on_states(starts_kernel, [state] * 2, now(to), ends, ends_other, state_in))
    gate_rest, there = [gate_end, gate_end_x], places_of(mirrored ^ 1)

    count = 2
    lent_parts = wait(*gate_with(borrowed, gate_rest, now(there), gate_begun, 0, scanned_lent, state_lent, norm_gain, count))
    backs = [along(now(part), OUTWARD) for part in lent_parts]
    mine_parts = wait(*gate_with(mine, gate_rest, now(there), gate_begun, 1, scanned_mine, state_mine, norm_gain, count))
    back0, far_x, both_x = wait(backs[0], far_x, both_x)
    pairs = [block.reshape(2, rows, width) for block in (out_both, both_x, far, far_x)]
    place_of = lambda index: jnp.where(
        index == plane, 0, jnp.where(index == partner, 1, jnp.where(index == jnp.where(lower, 2, 1), 2, 3))
    )

    def products_of(part, back, *flips):
        at = jnp.stack([place_of(head_block ^ flip) for flip in flips] + [middle.astype(jnp.int32)])
        return wait(*output_parts(mine_parts[part], back, pairs, now(at)))

    by3, by1 = products_of(0, back0, 3, 1)
    sent3, sent1 = across(now(by3), 3), across(now(by1), 1)
    by2, top = products_of(0, back0, 2, 0)
    sent2 = across(now(by2), 2)
    back1 = wait(backs[1])
    by3, by1, by2, bottom = products_of(1, back1, 3, 1, 2, 0)
    sent3, sent1, sent2 = wait(sent3, sent1, sent2)
    next3, next1, next2 = across(now(by3), 3), across(now(by1), 1), across(now(by2), 2)
    result = wait(sum_part([top, sent1, sent2, sent3], 0, count, to))
    return sum_part([bottom, next1, next2, next3], 1, count, now(to), result)


def sum_kernel(at_ref, *refs):
    blocks, out_ref = refs[:4], refs[-1]
    tokens, width = out_ref.shape
    f32 = jnp.float32
    squares = sum(block[tokens:].astype(f32) for block in blocks)
    row = (squares[:1] + squares[1:2])[:, :tokens]
    norm = lax.rsqrt(row / INNER + 1e-05)
    norm = jnp.broadcast_to(norm, (LANES, tokens)).T[:, :1]
    own_first = at_ref[at_ref.shape[0] - 2] == 0
    half = width // 2
    low, high = [
        sum(block[:tokens, columns].astype(f32) for block in blocks) * norm for columns in (slice(0, half), slice(half, width))
    ]
    out_ref[:, :half] = jnp.where(own_first, low, high).astype(out_ref.dtype)
    out_ref[:, half:] = jnp.where(own_first, high, low).astype(out_ref.dtype)


def sum_part(blocks, part, count, at, result=None):
    height, width = blocks[0].shape
    tokens = height - HALO
    vmem = pl.BlockSpec(memory_space=pltpu.VMEM)
    return pl.pallas_call(
        sum_kernel,
        grid=(1,),
        in_specs=[pl.BlockSpec(memory_space=pltpu.SMEM)]
        + [vmem] * len(blocks)
        + ([pl.BlockSpec(memory_space=pl.ANY)] if part else []),
        out_specs=pl.BlockSpec((tokens, width), lambda i: (part, 0)),
        out_shape=jax.ShapeDtypeStruct((tokens * count, width), jnp.bfloat16),
        input_output_aliases={1 + len(blocks): 0} if part else {},
        compiler_params=pltpu.CompilerParams(vmem_limit_bytes=VMEM),
        cost_estimate=pl.CostEstimate(flops=1, bytes_accessed=32 * tokens * width * count, transcendentals=0),
        name="sum_part",
    )(at, *blocks, *([result] if part else []))


def split_scan(results):
    return results[:3], results[3], results[4]


def plan_of(mesh):
    planes = mesh.shape["seq"] // CORES
    return local_paired if planes == 4 and mesh.shape["hid"] == planes else local_general


def solution(mesh):
    in_specs = (
        P("seq", None),
        P("seq", "hid"),
        P("seq", "hid"),
        P("seq", None),
        P("seq", None),
        P("seq", "hid"),
        P(None, "hid"),
        P(),
        P("hid"),
        P("hid"),
        P("hid"),
        P("hid"),
    )
    out_specs = P("seq", "hid")
    return jax.shard_map(plan_of(mesh), mesh=mesh, in_specs=in_specs, out_specs=out_specs, check_vma=False)
```

```python
import functools

import jax
import jax.numpy as jnp
from jax import lax
from jax.experimental import pallas as pl
from jax.experimental.pallas import tpu as pltpu
from jax.sharding import PartitionSpec as P

HEADS = 64
P_SIZE = 64
N = 128
G = 4
Q = 256
K = 4
INNER = 4096


def from_behind(block, axis, distance):
    devices = range(lax.axis_size(axis))
    route = [(i - distance, i) for i in devices if i - distance in devices]
    return lax.ppermute(block, axis, route)


def carried_in(array, axis, join, neutral):
    place = lax.axis_index(axis)
    gathered = jax.tree.map(
        lambda a, kind: lax.all_gather(a.astype(kind), axis), array, (jnp.bfloat16, jnp.bfloat16)
    )
    state = jax.tree.map(lambda a, e: jnp.zeros_like(a) + jnp.asarray(e, a.dtype), array, neutral)

    def one(step, state):
        return join(
            state,
            jax.tree.map(
                lambda a, own: lax.dynamic_index_in_dim(a, step, 0, False).astype(own.dtype),
                gathered,
                array,
            ),
        )

    return lax.fori_loop(0, place, one, state)


def causal_conv(values, before, kernel):
    length = values.shape[0]
    extended = jnp.concatenate([before, values], axis=0)
    summed = jnp.zeros(values.shape, jnp.float32)
    for position in range(kernel.shape[0]):
        summed = (
            summed + extended[position : position + length].astype(jnp.float32) * kernel[position]
        )
    return jax.nn.silu(summed).astype(jnp.bfloat16)


def combine_states(earlier, later):
    return (earlier[0] * later[0], later[0][:, None, None] * earlier[1] + later[1])


def roll_state(state, inputs):
    total_here, fresh_here = inputs
    return (jnp.exp(total_here)[:, None, None] * state + fresh_here, state)


def local_general(
    activations,
    w_inner,
    w_gate,
    w_groups,
    w_step,
    w_out,
    conv_inner,
    conv_groups,
    step_bias,
    decay_log,
    skip_gain,
    norm_gain,
):
    tok_rows = activations.shape[0]
    heads_dev = step_bias.shape[0]
    width_dev = w_inner.shape[1]
    head_block = lax.axis_index("hid")
    group_cols = 2 * N
    group_index = head_block * heads_dev // (HEADS // G)
    step_cols = lax.dynamic_slice_in_dim(w_step, head_block * heads_dev, heads_dev, 1)
    own_cols = lax.dynamic_slice_in_dim(w_groups, group_index * group_cols, group_cols, 1)
    piece_inner = lax.all_gather(w_inner, "seq", axis=0, tiled=True)
    piece_gate = lax.all_gather(w_gate, "seq", axis=0, tiled=True)
    piece_groups = lax.all_gather(own_cols, "seq", axis=0, tiled=True)
    piece_step = lax.all_gather(step_cols, "seq", axis=0, tiled=True)
    piece_out = lax.all_gather(w_out, "seq", axis=0, tiled=True)
    acc_inner = jnp.dot(activations, piece_inner, preferred_element_type=jnp.float32)
    acc_gate = jnp.dot(activations, piece_gate, preferred_element_type=jnp.float32)
    acc_groups = jnp.dot(activations, piece_groups, preferred_element_type=jnp.float32)
    acc_step = jnp.dot(activations, piece_step, preferred_element_type=jnp.float32)
    groups_in = acc_groups.astype(jnp.bfloat16)
    inner_in = acc_inner.astype(jnp.bfloat16)
    gate_in = acc_gate.astype(jnp.bfloat16)
    own_out_rows = lax.all_to_all(piece_out, "hid", split_axis=0, concat_axis=1, tiled=True)
    conv_group = lax.dynamic_slice_in_dim(conv_groups, group_index * group_cols, group_cols, 1)
    tail_rows = K - 1
    inner_prev, groups_prev = from_behind(
        (inner_in[tok_rows - tail_rows :], groups_in[tok_rows - tail_rows :]), "seq", 1
    )
    inner_conv = causal_conv(inner_in, inner_prev, conv_inner)
    groups_conv = causal_conv(groups_in, groups_prev, conv_group)
    step_size = jax.nn.softplus(acc_step + step_bias)
    rates = -jnp.exp(decay_log)
    span_count = tok_rows // Q
    heads_x = inner_conv.reshape(span_count, Q, heads_dev, P_SIZE)
    b_in = groups_conv[:, :N].reshape(span_count, Q, N)
    c_out = groups_conv[:, N:].reshape(span_count, Q, N)
    block_dt = step_size.reshape(span_count, Q, heads_dev)
    cum_decay = jnp.cumsum(block_dt * rates, axis=1)
    scores = jnp.einsum("ctn,csn->cts", c_out, b_in, preferred_element_type=jnp.float32)
    ahead = jnp.arange(Q)[:, None] >= jnp.arange(Q)[None, :]
    decay_t = jnp.swapaxes(cum_decay, 1, 2)
    gap = jnp.where(ahead, decay_t[:, :, :, None] - decay_t[:, :, None, :], -1e30)
    mixing = (scores[:, None] * jnp.exp(gap) * jnp.swapaxes(block_dt, 1, 2)[:, :, None, :]).astype(
        jnp.bfloat16
    )
    intra = jnp.einsum("chts,cshp->cthp", mixing, heads_x, preferred_element_type=jnp.float32)
    span_total = cum_decay[:, -1]
    weights_in = jnp.exp(span_total[:, None, :] - cum_decay) * block_dt
    weighted = (b_in[:, :, None, :] * weights_in[:, :, :, None]).astype(jnp.bfloat16)
    fresh = jnp.einsum("cshn,cshp->chnp", weighted, heads_x, preferred_element_type=jnp.float32)
    zero_state = jnp.zeros((heads_dev, N, P_SIZE), jnp.float32)
    local_end, starts = lax.scan(roll_state, zero_state, (span_total, fresh))
    log_total = jnp.sum(span_total, axis=0)
    prior = jnp.cumsum(span_total, axis=0) - span_total
    identity = (jnp.ones((heads_dev,), jnp.float32), zero_state)
    state_in = carried_in((jnp.exp(log_total), local_end), "seq", combine_states, identity)[1]
    span_in = starts + jnp.exp(prior)[:, :, None, None] * state_in[None]
    inter = jnp.einsum(
        "ctn,chnp->cthp", c_out.astype(jnp.float32), span_in, precision=lax.Precision.HIGHEST
    )
    inter = inter * jnp.exp(cum_decay)[:, :, :, None]
    mixed = (intra + inter).reshape(tok_rows, width_dev) + jnp.repeat(
        skip_gain, P_SIZE
    ) * inner_conv.astype(jnp.float32)
    gated = mixed * jax.nn.silu(gate_in.astype(jnp.float32))
    squares = lax.psum(jnp.sum(gated * gated, axis=1), "hid")
    normed = (gated * lax.rsqrt(squares / INNER + 1e-05)[:, None] * norm_gain).astype(jnp.bfloat16)
    start_sum = jnp.zeros((tok_rows, own_out_rows.shape[0]), jnp.float32)
    total = start_sum
    piece = lax.all_gather(normed, "hid", axis=1, tiled=True)
    block_count = piece.shape[1] // width_dev
    for block in range(block_count):
        cols = piece[:, block * width_dev : (block + 1) * width_dev]
        weight_cols = lax.dynamic_slice_in_dim(own_out_rows, block * width_dev, width_dev, 1)
        partial_out = lax.dot_general(
            cols, weight_cols, (((1,), (1,)), ((), ())), preferred_element_type=jnp.float32
        )
        total = total + lax.optimization_barrier(partial_out.astype(jnp.bfloat16)).astype(
            jnp.float32
        )
    return total.astype(jnp.bfloat16)


CORES = 2
HALO = 16
LANES = 128
VMEM = 28 * 1024 * 1024
COST = pl.CostEstimate(flops=1, bytes_accessed=1, transcendentals=0)


def both_cores(moves):
    return [(CORES * a + c, CORES * b + c) for a, b in moves for c in range(CORES)]


INWARD = both_cores([(0, 1), (3, 2)])
OUTWARD = both_cores([(1, 0), (2, 3)])
MIDDLE = both_cores([(1, 2), (2, 1)])
MIDDLE_UP = both_cores([(1, 2)])
NEAR = INWARD + OUTWARD


def other_core(block):
    return lax.ppermute(block, "seq", [(i, i ^ 1) for i in range(lax.axis_size("seq"))])


def along(block, route):
    return lax.ppermute(block, "seq", route)


def across(block, flip):
    return lax.ppermute(block, "hid", [(i, i ^ flip) for i in range(lax.axis_size("hid"))])


def silu(v):
    return v / (1.0 + jnp.exp(-v))


def convolved(window, taps, rows):
    summed = window[HALO : HALO + rows] * taps[K - 1 : K]
    for position in range(K - 1):
        shifted = pltpu.roll(window, K - 1 - position, 0)
        summed = summed + shifted[HALO : HALO + rows] * taps[position : position + 1]
    return silu(summed).astype(jnp.bfloat16)


def pair_of(low_half, left, right):
    return jnp.where(low_half, left, right)


def scan_kernel(
    first_ref, step_ref, taps_ref, group_taps_ref, bias_ref, decay_ref, skip_ref,
    y_ref, c_ref, grown_ref, end_ref, through_ref, prior_ref,
):
    span = pl.program_id(0)
    f32, bf16 = jnp.float32, jnp.bfloat16
    exact = lax.Precision.HIGHEST
    half = Q // 2

    @pl.when(span == 0)
    def _():
        end_ref[...] = jnp.zeros_like(end_ref)
        prior_ref[...] = jnp.zeros_like(prior_ref)

    width = y_ref.shape[1]
    rows = pl.ds(pl.multiple_of(span * Q, Q), Q + HALO)
    rounded = lambda columns: first_ref[rows, columns].astype(f32)
    groups = convolved(rounded(slice(width, width + 2 * N)), group_taps_ref[...], Q)
    b_in, c_out = groups[:, :N], groups[:, N:]
    c_ref[...] = c_out
    scores = lax.dot_general(c_out, b_in, (((1,), (1,)), ((), ())), preferred_element_type=f32)
    t_at = lax.broadcasted_iota(jnp.int32, (Q, Q), 0)
    s_at = lax.broadcasted_iota(jnp.int32, (Q, Q), 1)
    ahead = t_at >= s_at
    scores = jnp.where(ahead, scores, 0.0)
    raw = step_ref[...] + bias_ref[...]
    step = jnp.maximum(raw, 0.0) + jnp.log1p(jnp.exp(-jnp.abs(raw)))
    rated = step * -jnp.exp(decay_ref[...])
    cum = jnp.dot(jnp.where(ahead, 1.0, 0.0), rated, precision=exact, preferred_element_type=f32)
    last = cum[Q - 1 : Q, :]
    prior = prior_ref[...]
    grown_ref[...] = jnp.exp(cum + prior)
    prior_ref[...] = prior + last
    through = jnp.exp(prior + last)
    cum_t, step_t = cum.T, step.T
    grow = jnp.exp(cum)
    weight = jnp.exp(last - cum) * step
    fade = jnp.exp(last)
    low = lax.broadcasted_iota(jnp.int32, (Q, LANES), 1) < P_SIZE
    per = LANES // P_SIZE
    for j in range(width // LANES):
        lanes = slice(j * LANES, (j + 1) * LANES)
        x = convolved(rounded(lanes), taps_ref[:, lanes], Q)
        x_wide = x.astype(f32)
        parts = []
        for h in (per * j, per * j + 1):
            col = cum[:, h : h + 1]
            row, scale = cum_t[h : h + 1, :], step_t[h : h + 1, :]
            top = scores[:half, :half] * jnp.exp(jnp.minimum(col[:half] - row[:, :half], 0.0)) * scale[:, :half]
            bottom = scores[half:] * jnp.exp(jnp.minimum(col[half:] - row, 0.0)) * scale
            parts.append(
                jnp.concatenate(
                    [
                        jnp.dot(top.astype(bf16), x[:half], preferred_element_type=f32),
                        jnp.dot(bottom.astype(bf16), x, preferred_element_type=f32),
                    ],
                    axis=0,
                )
            )
        y = pair_of(low, parts[0], parts[1])
        a, b = per * j, per * j + 1
        state = end_ref[:, lanes]
        high = state.astype(bf16)
        rest = (state - high.astype(f32)).astype(bf16)
        carried = jnp.dot(c_out, high, preferred_element_type=f32) + jnp.dot(c_out, rest, preferred_element_type=f32)
        y = y + carried * pair_of(low, grow[:, a : a + 1], grow[:, b : b + 1])
        y_ref[:, lanes] = y + x_wide * skip_ref[:, lanes]
        weighted = (x_wide * pair_of(low, weight[:, a : a + 1], weight[:, b : b + 1])).astype(bf16)
        fresh = lax.dot_general(b_in, weighted, (((0,), (0,)), ((), ())), preferred_element_type=f32)
        end_ref[:, lanes] = state * pair_of(low[:1], fade[:, a : a + 1], fade[:, b : b + 1]) + fresh
        through_ref[:, lanes] = pair_of(low[:1], through[:, a : a + 1], through[:, b : b + 1])


def scan_segment(first, step, taps, group_taps, bias, decay, skip):
    tokens, width = step.shape[0], taps.shape[1]
    whole = lambda a: pl.BlockSpec(a.shape, lambda i: (0,) * a.ndim)
    spans = lambda w: pl.BlockSpec((Q, w), lambda i: (i, 0))
    fixed = lambda shape: pl.BlockSpec(shape, lambda i: (0, 0))
    f32 = jnp.float32
    return pl.pallas_call(
        scan_kernel,
        grid=(tokens // Q,),
        in_specs=[whole(first), spans(LANES)] + [whole(a) for a in (taps, group_taps, bias, decay, skip)],
        out_specs=[spans(width), spans(N), spans(LANES), fixed((N, width)), fixed((1, width))],
        out_shape=[
            jax.ShapeDtypeStruct((tokens, width), f32),
            jax.ShapeDtypeStruct((tokens, N), jnp.bfloat16),
            jax.ShapeDtypeStruct((tokens, LANES), f32),
            jax.ShapeDtypeStruct((N, width), f32),
            jax.ShapeDtypeStruct((1, width), f32),
        ],
        scratch_shapes=[pltpu.VMEM((1, LANES), f32)],
        compiler_params=pltpu.CompilerParams(vmem_limit_bytes=VMEM),
        cost_estimate=COST,
        name="scan_segment",
    )(first, step, taps, group_taps, bias, decay, skip)


def fetch(at_ref, sources, pieces, source_buf, piece_buf, sems):
    rows = piece_buf.shape[1]
    each = source_buf.shape[1] // len(sources)
    waits = []
    for piece in pieces:
        for part in range(piece.shape[0] // rows):
            i = len(waits)
            columns = pl.ds(pl.multiple_of(at_ref[i] * rows, rows), rows)
            copies = [pltpu.make_async_copy(piece.at[pl.ds(part * rows, rows)], piece_buf.at[i], sems.at[i, 0])]
            for k, source in enumerate(sources):
                first = source.shape[0] - each
                copies.append(
                    pltpu.make_async_copy(
                        source.at[pl.ds(first, each), columns], source_buf.at[i, pl.ds(k * each, each)], sems.at[i, 1 + k]
                    )
                )
            for copy in copies:
                copy.start()
            waits.append(lambda copies=copies: [copy.wait() for copy in copies])
    return waits


def blocks_of(width):
    step = 2 * LANES
    return [slice(n, min(n + step, width)) for n in range(0, width, step)]


def project_kernel(n_sources, count, begun, final, at_ref, *refs):
    sources, pieces, refs = refs[:n_sources], refs[n_sources : n_sources + count], refs[n_sources + count :]
    partial_ref, refs = (refs[0], refs[1:]) if begun else (None, refs)
    outs, (total_ref, source_buf, piece_buf, sems) = refs[:-4], refs[-4:]
    waits = fetch(at_ref, sources, pieces, source_buf, piece_buf, sems)
    for i in range(0, len(waits), 2):
        waits[i]()
        waits[i + 1]()
        for columns in blocks_of(total_ref.shape[1]):
            term = jnp.dot(source_buf[i], piece_buf[i, :, columns], preferred_element_type=jnp.float32)
            term = term + jnp.dot(source_buf[i + 1], piece_buf[i + 1, :, columns], preferred_element_type=jnp.float32)
            if i or begun:
                term = term + (total_ref if i else partial_ref)[:, columns]
            total_ref[:, columns] = term
    if final:
        outs[0][...] = total_ref[:, : outs[0].shape[1]].astype(outs[0].dtype)
        outs[1][...] = total_ref[HALO:, outs[0].shape[1] :]


def project(sources, tokens, pieces, places, rows, partial=None, final=False):
    steps, width = places.shape[0], pieces[0].shape[1]
    height = tokens * len(sources)
    f32 = jnp.float32
    if final:
        out_shape = [
            jax.ShapeDtypeStruct((height, width - LANES), jnp.bfloat16),
            jax.ShapeDtypeStruct((height - HALO, LANES), f32),
        ]
    else:
        out_shape = jax.ShapeDtypeStruct((height, width), f32)
    total = [pltpu.VMEM((height, width), f32)] if final else []
    kernel = functools.partial(project_kernel, len(sources), len(pieces), partial is not None, final)

    def body(*refs):
        if final:
            kernel(*refs)
        else:
            kernel(*refs[:-4], *refs[-4:])

    vmem = pl.BlockSpec(memory_space=pltpu.VMEM)
    return pl.pallas_call(
        body,
        in_specs=[pl.BlockSpec(memory_space=pltpu.SMEM)]
        + [pl.BlockSpec(memory_space=pl.ANY)] * (len(sources) + len(pieces))
        + ([vmem] if partial is not None else []),
        out_specs=[vmem] * 2 if final else vmem,
        out_shape=out_shape,
        scratch_shapes=total
        + [
            pltpu.VMEM((steps, height, rows), jnp.bfloat16),
            pltpu.VMEM((steps, rows, width), jnp.bfloat16),
            pltpu.SemaphoreType.DMA((steps, 1 + len(sources))),
        ],
        compiler_params=pltpu.CompilerParams(vmem_limit_bytes=VMEM),
        cost_estimate=COST,
        name="project",
    )(places, *sources, *pieces, *([partial] if partial is not None else []))


def two_rows(row, height):
    high = row.astype(jnp.bfloat16).astype(jnp.float32)
    at = lax.broadcasted_iota(jnp.int32, (height, row.shape[1]), 0)
    return jnp.where(at == 0, high, jnp.where(at == 1, row - high, 0.0)).astype(jnp.bfloat16)


def gate_kernel(count, at_ref, source_ref, *refs):
    pieces, refs = refs[:count], refs[count:]
    begun_ref, y_ref, c_ref, grown_ref, state_ref, gain_ref, *outs, source_buf, piece_buf, sems = refs
    f32, bf16 = jnp.float32, jnp.bfloat16
    waits = fetch(at_ref, [source_ref], pieces, source_buf, piece_buf, sems)
    c_out, grown = c_ref[...], grown_ref[...]
    grown_high = grown.astype(bf16)
    grown_rest = (grown - grown_high.astype(f32)).astype(bf16)
    squares = None
    share = y_ref.shape[0] // len(outs)
    for n, columns in enumerate(blocks_of(y_ref.shape[1])):
        block = columns.stop - columns.start
        total = begun_ref[:, columns]
        for i in range(len(waits)):
            if n == 0:
                waits[i]()
            total = total + jnp.dot(source_buf[i], piece_buf[i, :, columns], preferred_element_type=f32)
        lane = lax.broadcasted_iota(jnp.int32, (LANES, block), 1) + columns.start
        of_head = jnp.where(lane // P_SIZE == lax.broadcasted_iota(jnp.int32, (LANES, block), 0), 1.0, 0.0).astype(bf16)
        spread = jnp.dot(grown_high, of_head, preferred_element_type=f32)
        spread = spread + jnp.dot(grown_rest, of_head, preferred_element_type=f32)
        state = state_ref[:, columns]
        high = state.astype(bf16)
        rest = (state - high.astype(f32)).astype(bf16)
        carried = jnp.dot(c_out, high, preferred_element_type=f32) + jnp.dot(c_out, rest, preferred_element_type=f32)
        gated = (y_ref[:, columns] + carried * spread) * silu(total.astype(bf16).astype(f32))
        scaled = (gated * gain_ref[:, columns]).astype(bf16)
        for k, out in enumerate(outs):
            out[:share, columns] = scaled[k * share : (k + 1) * share]
        square = gated * gated
        for k in range(block // LANES):
            part = square[:, k * LANES : (k + 1) * LANES]
            squares = part if squares is None else squares + part
    ones = jnp.ones((8, LANES), f32)
    for k, out in enumerate(outs):
        part = squares[k * share : (k + 1) * share]
        row = lax.dot_general(
            ones, part, (((1,), (1,)), ((), ())), precision=lax.Precision.HIGHEST, preferred_element_type=f32
        )[:1]
        row = jnp.concatenate([row, jnp.zeros((1, out.shape[1] - share), f32)], axis=1)
        out[share:] = two_rows(row, out.shape[0] - share)


def gate_with(source, pieces, places, begun, part, scanned, state, gain, parts):
    y, c_out, grown = scanned
    tokens, width = y.shape
    steps = places.shape[0]
    rows = sum(piece.shape[0] for piece in pieces) // steps
    vmem = pl.BlockSpec(memory_space=pltpu.VMEM)
    return pl.pallas_call(
        functools.partial(gate_kernel, len(pieces)),
        grid=(1,),
        in_specs=[pl.BlockSpec(memory_space=pltpu.SMEM)]
        + [pl.BlockSpec(memory_space=pl.ANY)] * (1 + len(pieces))
        + [pl.BlockSpec((tokens, width), lambda i: (part, 0))]
        + [vmem] * 5,
        out_specs=[vmem] * parts,
        out_shape=[jax.ShapeDtypeStruct((tokens // parts + HALO, width), jnp.bfloat16)] * parts,
        scratch_shapes=[
            pltpu.VMEM((steps, tokens, rows), jnp.bfloat16),
            pltpu.VMEM((steps, rows, width), jnp.bfloat16),
            pltpu.SemaphoreType.DMA((steps, 2)),
        ],
        compiler_params=pltpu.CompilerParams(vmem_limit_bytes=VMEM),
        cost_estimate=COST,
        name="gate",
    )(places, source, *pieces, begun, y, c_out, grown, state, gain[None, :])


def output_kernel(at_ref, here_ref, back_ref, *refs):
    weights, outs, (block_buf, weight_buf, sems) = refs[:4], refs[4:-3], refs[-3:]
    features = weight_buf.shape[1]
    tokens = block_buf.shape[0] - HALO
    here = pltpu.make_async_copy(here_ref, block_buf, sems.at[2 * len(outs)])
    back = pltpu.make_async_copy(back_ref, block_buf, sems.at[2 * len(outs)])
    stays = at_ref[len(outs)] == 1
    pl.when(stays)(here.start)
    pl.when(jnp.logical_not(stays))(back.start)
    waits = []
    for j in range(len(outs)):
        for i in range(2):
            slot = 2 * j + i
            index, is_near = at_ref[j] % 2, at_ref[j] < 2
            near, far = [pltpu.make_async_copy(weights[k + i].at[index], weight_buf.at[slot], sems.at[slot]) for k in (0, 2)]
            pl.when(is_near)(near.start)
            pl.when(jnp.logical_not(is_near))(far.start)
            waits.append((is_near, near, far))
    pl.when(stays)(here.wait)
    pl.when(jnp.logical_not(stays))(back.wait)
    for j, out in enumerate(outs):
        out[tokens:] = block_buf[tokens:]
        for i in range(2):
            is_near, near, far = waits[2 * j + i]
            pl.when(is_near)(near.wait)
            pl.when(jnp.logical_not(is_near))(far.wait)
            product = lax.dot_general(
                block_buf[:tokens], weight_buf[2 * j + i], (((1,), (1,)), ((), ())), preferred_element_type=jnp.float32
            )
            out[:tokens, i * features : (i + 1) * features] = product.astype(out.dtype)


def output_parts(here, back, pairs, at):
    height, width = here.shape
    features, count = pairs[0].shape[1], at.shape[0] - 1
    vmem, anywhere = pl.BlockSpec(memory_space=pltpu.VMEM), pl.BlockSpec(memory_space=pl.ANY)
    return pl.pallas_call(
        output_kernel,
        in_specs=[pl.BlockSpec(memory_space=pltpu.SMEM)] + [anywhere] * 6,
        out_specs=[vmem] * count,
        out_shape=[jax.ShapeDtypeStruct((height, 2 * features), jnp.bfloat16)] * count,
        scratch_shapes=[
            pltpu.VMEM((height, width), jnp.bfloat16),
            pltpu.VMEM((2 * count, features, width), jnp.bfloat16),
            pltpu.SemaphoreType.DMA((2 * count + 1,)),
        ],
        compiler_params=pltpu.CompilerParams(vmem_limit_bytes=VMEM),
        cost_estimate=COST,
        name="output_parts",
    )(at, here, back, *pairs)


def pack_kernel(at_ref, mine_ref, lent_ref, mine_fade_ref, lent_fade_ref, out_ref):
    lent_first = at_ref[at_ref.shape[0] - 1] == 1
    for which in range(2):
        pick = lent_first if which == 0 else jnp.logical_not(lent_first)
        out_ref[which, :N] = jnp.where(pick, lent_ref[...], mine_ref[...]).astype(out_ref.dtype)
        out_ref[which, N:] = two_rows(jnp.where(pick, lent_fade_ref[...], mine_fade_ref[...]), out_ref.shape[1] - N)


def segments_of(at_ref, own_ref, other_ref):
    core = at_ref[at_ref.shape[0] - 2]
    for which in range(2):
        for c in range(CORES):
            read = lambda rows: jnp.where(
                core == c, own_ref[which, rows].astype(jnp.float32), other_ref[which, rows].astype(jnp.float32)
            )
            fade = read(slice(N, N + HALO))
            yield which, c, fade[:1] + fade[1:2], read(slice(0, N))


def through_kernel(at_ref, own_ref, other_ref, out_ref):
    state = None
    for _, _, fade, end in segments_of(at_ref, own_ref, other_ref):
        state = end if state is None else fade * state + end
    out_ref[...] = state.astype(out_ref.dtype)


def starts_kernel(at_ref, own_ref, other_ref, before_ref, mine_ref, lent_ref):
    lent_first, core = at_ref[at_ref.shape[0] - 1] == 1, at_ref[at_ref.shape[0] - 2]
    state = before_ref[...].astype(jnp.float32)
    for which, c, fade, end in segments_of(at_ref, own_ref, other_ref):
        to_lent = lent_first if which == 0 else jnp.logical_not(lent_first)

        @pl.when((core == c) & to_lent)
        def _(state=state):
            lent_ref[...] = state

        @pl.when((core == c) & jnp.logical_not(to_lent))
        def _(state=state):
            mine_ref[...] = state

        state = fade * state + end


def on_states(kernel, shapes, at, *arrays):
    vmem = pl.BlockSpec(memory_space=pltpu.VMEM)
    return pl.pallas_call(
        kernel,
        in_specs=[pl.BlockSpec(memory_space=pltpu.SMEM)] + [vmem] * len(arrays),
        out_specs=[vmem] * len(shapes),
        out_shape=shapes,
        compiler_params=pltpu.CompilerParams(vmem_limit_bytes=VMEM),
        cost_estimate=COST,
        name="states",
    )(at, *arrays)


def arrange_kernel(moves, count, at_ref, *refs):
    sources, outs, sems = refs[:count], refs[count:-1], refs[-1]
    copies = []
    for k, (source, rows, out, place, condition) in enumerate(moves):
        copy = pltpu.make_async_copy(sources[source].at[rows], outs[out].at[place(at_ref)], sems.at[k])
        copies.append((copy, condition))
    for copy, condition in copies:
        copy.start() if condition is None else pl.when(condition(at_ref))(copy.start)
    for copy, condition in copies:
        copy.wait() if condition is None else pl.when(condition(at_ref))(copy.wait)


def arrange(sources, shapes, moves, at):
    anywhere = pl.BlockSpec(memory_space=pl.ANY)
    return pl.pallas_call(
        functools.partial(arrange_kernel, moves, len(sources)),
        in_specs=[pl.BlockSpec(memory_space=pltpu.SMEM)] + [anywhere] * len(sources),
        out_specs=[pl.BlockSpec(memory_space=pltpu.VMEM)] * len(shapes),
        out_shape=[jax.ShapeDtypeStruct(shape, sources[0].dtype) for shape in shapes],
        scratch_shapes=[pltpu.SemaphoreType.DMA((len(moves),))],
        compiler_params=pltpu.CompilerParams(vmem_limit_bytes=VMEM),
        cost_estimate=COST,
        name="arrange",
    )(at, *sources)


def stacked(blocks, at):
    moves, first = [], 0
    for k, block in enumerate(blocks):
        rows = slice(first, first + block.shape[0])
        moves.append((k, slice(None), 0, lambda at_ref, rows=rows: rows, None))
        first = rows.stop
    return arrange(blocks, [(first,) + blocks[0].shape[1:]], moves, at)[0]


class Order:
    def __init__(self, token):
        self.token = token

    def wait(self, *blocks):
        self.token, *blocks = lax.optimization_barrier((self.token, *blocks))
        return blocks[0] if len(blocks) == 1 else blocks

    def now(self, block):
        return lax.optimization_barrier((block, self.token))[0]


def local_paired(
    activations, w_inner, w_gate, w_groups, w_step, w_out, conv_inner, conv_groups, step_bias, decay_log, skip_gain, norm_gain
):
    f32, bf16 = jnp.float32, jnp.bfloat16
    tokens, depth = activations.shape
    heads_dev = step_bias.shape[0]
    width = w_inner.shape[1]
    place, head_block = lax.axis_index("seq"), lax.axis_index("hid")
    plane, core = place // CORES, place % CORES
    lower = plane < 2
    middle = (plane == 1) | (plane == 2)
    group_cols = 2 * N
    group_index = head_block * heads_dev // (HEADS // G)
    pad = LANES - heads_dev
    devices, chips = lax.axis_size("seq"), lax.axis_size("hid")
    half = tokens // 2
    order = Order(step_bias)
    now, wait = order.now, order.wait

    kept_tokens = K
    folded = activations[tokens - kept_tokens :].reshape(HALO, kept_tokens * depth // HALO)
    w_first = jnp.concatenate(
        [
            w_inner,
            lax.dynamic_slice_in_dim(w_groups, group_index * group_cols, group_cols, 1),
            jnp.pad(lax.dynamic_slice_in_dim(w_step, head_block * heads_dev, heads_dev, 1), ((0, 0), (0, pad))),
        ],
        axis=1,
    )
    w_first = jnp.concatenate([w_first, jnp.pad(folded, ((0, 0), (0, w_first.shape[1] - folded.shape[1])))], axis=0)
    tail_of = lambda block: block[block.shape[0] - HALO :, : folded.shape[1]]
    unfolded = lambda tail: jnp.pad(tail.reshape(kept_tokens, depth), ((HALO - kept_tokens, 0), (0, 0)))
    quarter = depth // chips

    mirrored = chips - 1 - plane
    partner = plane ^ 1
    places_of = lambda *planes: jnp.stack([jnp.clip(p, 0, chips - 1) * CORES + c for p in planes for c in (core, 1 - core)])
    early, late = places_of(plane, mirrored), places_of(partner, mirrored ^ 1)
    group_taps = lax.dynamic_slice_in_dim(conv_groups, group_index * group_cols, group_cols, 1)
    lane_row = lambda v: jnp.pad(v, (0, pad))[None, :]
    consts = (conv_inner, group_taps, lane_row(step_bias), lane_row(decay_log), jnp.repeat(skip_gain, P_SIZE)[None, :])
    rows = w_out.shape[0]
    to = jnp.stack([head_block ^ flip for flip in range(chips)] + [middle.astype(jnp.int32), core, lower.astype(jnp.int32)])
    first_out, first_far = along(w_first, INWARD), along(w_first, MIDDLE)
    lent = lax.dynamic_slice_in_dim(activations, head_block * quarter, quarter, 1)
    first_x, gate_x, lent = wait(other_core(w_first), other_core(w_gate), lent)
    lent_here = along(now(lent), INWARD)
    first_far, first_out = wait(first_far, first_out)
    first_end, near = along(now(first_out), MIDDLE), along(now(w_out), NEAR)
    far_x, out_x = wait(other_core(now(first_far)), other_core(now(first_out)))
    tail_x, tail_far, tail_out = tail_of(first_x), tail_of(far_x), tail_of(out_x)
    halo = unfolded(jnp.where(core == 1, tail_x, jnp.where(plane == 1, tail_out, tail_far)))
    halo_lent = unfolded(jnp.where(core == 1, tail_out, jnp.where(plane == 1, jnp.zeros_like(tail_x), tail_x)))
    mine, halo_lent = wait(stacked([halo, activations], now(to)), halo_lent)
    first_early = [w_first, first_x, first_far, far_x]
    begun_mine, lent_here = wait(project([mine], tokens + HALO, first_early, now(early), rows), lent_here)
    lent_x, lent_y, out_far = across(now(lent_here), 1), across(now(lent_here), 2), along(now(w_out), MIDDLE)
    first_end, near, lent_x, lent_y, out_far = wait(first_end, near, lent_x, lent_y, out_far)
    end_x, out_end = other_core(now(first_end)), along(now(near), MIDDLE)
    by_x, by_y = wait(
        *arrange(
            [lent_y, lent_x],
            [(half, quarter), (tokens - half, quarter)],
            [
                (0, slice(0, half), 0, lambda at: slice(None), None),
                (1, slice(half, tokens), 1, lambda at: slice(None), None),
            ],
            now(to),
        )
    )
    by_x, by_y = across(now(by_x), 1), across(now(by_y), 2)
    end_x = wait(end_x)
    gate_far, gate_out = along(now(w_gate), MIDDLE), along(now(w_gate), INWARD)
    first_late = [first_out, out_x, first_end, end_x]
    first_mine, step_mine, by_x, by_y = wait(
        *project([mine], tokens + HALO, first_late, now(late), rows, begun_mine, True), by_x, by_y
    )
    out_far_on = along(now(out_far), OUTWARD)
    columns = lambda flip, first, last: lambda at: (slice(HALO + first, HALO + last), pl.ds(at[flip] * quarter, quarter))
    (borrowed,) = arrange(
        [halo_lent, lent_here, lent_x, lent_y, by_x, by_y],
        [(HALO + tokens, depth)],
        [(0, slice(None), 0, lambda at: slice(0, HALO), None)]
        + [(1 + flip, slice(None), 0, columns(flip, 0, tokens), None) for flip in range(3)]
        + [(4, slice(None), 0, columns(3, 0, half), None), (5, slice(None), 0, columns(3, half, tokens), None)],
        now(to),
    )
    borrowed = wait(borrowed)
    first_lent, step_lent = wait(
        *project([borrowed], tokens + HALO, first_early + first_late, now(jnp.concatenate([early, late])), rows, None, True)
    )
    scanned_lent, end_lent, through_lent = split_scan(wait(*scan_segment(now(first_lent), step_lent, *consts)))
    scanned_mine, end_mine, through_mine = split_scan(wait(*scan_segment(now(first_mine), step_mine, *consts)))
    out_end, gate_out, gate_far, out_far_on = wait(out_end, gate_out, gate_far, out_far_on)
    out_end_on, gate_end = along(now(out_end), OUTWARD), along(now(gate_out), MIDDLE)
    gate_out_x, gate_far_x = other_core(now(gate_out)), other_core(now(gate_far))

    state = jax.ShapeDtypeStruct((N, width), f32)
    (ends,) = on_states(
        pack_kernel, [jax.ShapeDtypeStruct((2, N + HALO, width), bf16)], now(to), end_mine, end_lent, through_mine, through_lent
    )
    ends = wait(ends)
    ends_other = wait(other_core(now(ends)))
    (run,) = wait(on_states(through_kernel, [jax.ShapeDtypeStruct((N, width), bf16)], now(to), ends, ends_other))
    state_in = along(now(run), MIDDLE_UP)
    gate_out_x, gate_far_x = wait(gate_out_x, gate_far_x)
    gate_early = [w_gate, gate_x, gate_out, gate_out_x, gate_far, gate_far_x]
    gate_begun = wait(project([borrowed, mine], tokens, gate_early, now(places_of(plane, partner, mirrored)), rows))
    gate_end, state_in, out_end_on = wait(gate_end, state_in, out_end_on)
    gate_end_x = other_core(now(gate_end))
    row = lambda index: lambda at: slice(index * rows, (index + 1) * rows)
    stays, goes = lambda at: at[chips] == 1, lambda at: at[chips] == 0
    both, far = wait(
        *arrange(
            [w_out, near, out_far, out_end, out_far_on, out_end_on],
            [(2 * rows, width)] * 2,
            [
                (0, slice(None), 0, row(0), None),
                (1, slice(None), 0, row(1), None),
                (2, slice(None), 1, row(0), stays),
                (3, slice(None), 1, row(1), stays),
                (4, slice(None), 1, row(0), goes),
                (5, slice(None), 1, row(1), goes),
            ],
            now(to),
        )
    )
    state_mine, state_lent, gate_end_x = wait(
        *on_states(starts_kernel, [state] * 2, now(to), ends, ends_other, state_in), gate_end_x
    )
    both_x, far_x = other_core(now(both)), other_core(now(far))
    gate_rest, there = [gate_end, gate_end_x], places_of(mirrored ^ 1)

    count = 2
    lent_parts = wait(*gate_with(borrowed, gate_rest, now(there), gate_begun, 0, scanned_lent, state_lent, norm_gain, count))
    backs = [along(now(part), OUTWARD) for part in lent_parts]
    mine_parts = wait(*gate_with(mine, gate_rest, now(there), gate_begun, 1, scanned_mine, state_mine, norm_gain, count))
    back0, far_x, both_x = wait(backs[0], far_x, both_x)
    pairs = [block.reshape(2, rows, width) for block in (both, both_x, far, far_x)]
    place_of = lambda index: jnp.where(
        index == plane, 0, jnp.where(index == partner, 1, jnp.where(index == jnp.where(lower, 2, 1), 2, 3))
    )

    def products_of(part, back, *flips):
        at = jnp.stack([place_of(head_block ^ flip) for flip in flips] + [middle.astype(jnp.int32)])
        return wait(*output_parts(mine_parts[part], back, pairs, now(at)))

    by3, by1, by2, top = products_of(0, back0, 3, 1, 2, 0)
    sent3, sent1, sent2 = across(now(by3), 3), across(now(by1), 1), across(now(by2), 2)
    back1 = wait(backs[1])
    by3, by1, by2, bottom = products_of(1, back1, 3, 1, 2, 0)
    sent3 = wait(sent3)
    next3 = across(now(by3), 3)
    sent1, sent2 = wait(sent1, sent2)
    next1, next2 = across(now(by1), 1), across(now(by2), 2)
    result = wait(sum_part([top, sent1, sent2, sent3], 0, count, to))
    return sum_part([bottom, next1, next2, next3], 1, count, now(to), result)


def sum_kernel(at_ref, *refs):
    blocks, out_ref = refs[:4], refs[-1]
    tokens, width = out_ref.shape
    f32 = jnp.float32
    squares = sum(block[tokens:].astype(f32) for block in blocks)
    row = (squares[:1] + squares[1:2])[:, :tokens]
    norm = lax.rsqrt(row / INNER + 1e-05)
    norm = jnp.broadcast_to(norm, (LANES, tokens)).T[:, :1]
    own_first = at_ref[at_ref.shape[0] - 2] == 0
    half = width // 2
    low, high = [
        sum(block[:tokens, columns].astype(f32) for block in blocks) * norm for columns in (slice(0, half), slice(half, width))
    ]
    out_ref[:, :half] = jnp.where(own_first, low, high).astype(out_ref.dtype)
    out_ref[:, half:] = jnp.where(own_first, high, low).astype(out_ref.dtype)


def sum_part(blocks, part, count, at, result=None):
    height, width = blocks[0].shape
    tokens = height - HALO
    vmem = pl.BlockSpec(memory_space=pltpu.VMEM)
    return pl.pallas_call(
        sum_kernel,
        grid=(1,),
        in_specs=[pl.BlockSpec(memory_space=pltpu.SMEM)]
        + [vmem] * len(blocks)
        + ([pl.BlockSpec(memory_space=pl.ANY)] if part else []),
        out_specs=pl.BlockSpec((tokens, width), lambda i: (part, 0)),
        out_shape=jax.ShapeDtypeStruct((tokens * count, width), jnp.bfloat16),
        input_output_aliases={1 + len(blocks): 0} if part else {},
        compiler_params=pltpu.CompilerParams(vmem_limit_bytes=VMEM),
        cost_estimate=pl.CostEstimate(flops=1, bytes_accessed=32 * tokens * width * count, transcendentals=0),
        name="sum_part",
    )(at, *blocks, *([result] if part else []))


def split_scan(results):
    return results[:3], results[3], results[4]


def plan_of(mesh):
    planes = mesh.shape["seq"] // CORES
    return local_paired if planes == 4 and mesh.shape["hid"] == planes else local_general


def solution(mesh):
    in_specs = (
        P("seq", None),
        P("seq", "hid"),
        P("seq", "hid"),
        P("seq", None),
        P("seq", None),
        P("seq", "hid"),
        P(None, "hid"),
        P(),
        P("hid"),
        P("hid"),
        P("hid"),
        P("hid"),
    )
    out_specs = P("seq", "hid")
    return jax.shard_map(plan_of(mesh), mesh=mesh, in_specs=in_specs, out_specs=out_specs, check_vma=False)
```

```python
import functools

import jax
import jax.numpy as jnp
from jax import lax
from jax.experimental import pallas as pl
from jax.experimental.pallas import tpu as pltpu
from jax.sharding import PartitionSpec as P

HEADS = 64
P_SIZE = 64
N = 128
G = 4
Q = 256
K = 4
INNER = 4096


def from_behind(block, axis, distance):
    devices = range(lax.axis_size(axis))
    route = [(i - distance, i) for i in devices if i - distance in devices]
    return lax.ppermute(block, axis, route)


def carried_in(array, axis, join, neutral):
    place = lax.axis_index(axis)
    gathered = jax.tree.map(
        lambda a, kind: lax.all_gather(a.astype(kind), axis), array, (jnp.bfloat16, jnp.bfloat16)
    )
    state = jax.tree.map(lambda a, e: jnp.zeros_like(a) + jnp.asarray(e, a.dtype), array, neutral)

    def one(step, state):
        return join(
            state,
            jax.tree.map(
                lambda a, own: lax.dynamic_index_in_dim(a, step, 0, False).astype(own.dtype),
                gathered,
                array,
            ),
        )

    return lax.fori_loop(0, place, one, state)


def causal_conv(values, before, kernel):
    length = values.shape[0]
    extended = jnp.concatenate([before, values], axis=0)
    summed = jnp.zeros(values.shape, jnp.float32)
    for position in range(kernel.shape[0]):
        summed = (
            summed + extended[position : position + length].astype(jnp.float32) * kernel[position]
        )
    return jax.nn.silu(summed).astype(jnp.bfloat16)


def combine_states(earlier, later):
    return (earlier[0] * later[0], later[0][:, None, None] * earlier[1] + later[1])


def roll_state(state, inputs):
    total_here, fresh_here = inputs
    return (jnp.exp(total_here)[:, None, None] * state + fresh_here, state)


def local_general(
    activations,
    w_inner,
    w_gate,
    w_groups,
    w_step,
    w_out,
    conv_inner,
    conv_groups,
    step_bias,
    decay_log,
    skip_gain,
    norm_gain,
):
    tok_rows = activations.shape[0]
    heads_dev = step_bias.shape[0]
    width_dev = w_inner.shape[1]
    head_block = lax.axis_index("hid")
    group_cols = 2 * N
    group_index = head_block * heads_dev // (HEADS // G)
    step_cols = lax.dynamic_slice_in_dim(w_step, head_block * heads_dev, heads_dev, 1)
    own_cols = lax.dynamic_slice_in_dim(w_groups, group_index * group_cols, group_cols, 1)
    piece_inner = lax.all_gather(w_inner, "seq", axis=0, tiled=True)
    piece_gate = lax.all_gather(w_gate, "seq", axis=0, tiled=True)
    piece_groups = lax.all_gather(own_cols, "seq", axis=0, tiled=True)
    piece_step = lax.all_gather(step_cols, "seq", axis=0, tiled=True)
    piece_out = lax.all_gather(w_out, "seq", axis=0, tiled=True)
    acc_inner = jnp.dot(activations, piece_inner, preferred_element_type=jnp.float32)
    acc_gate = jnp.dot(activations, piece_gate, preferred_element_type=jnp.float32)
    acc_groups = jnp.dot(activations, piece_groups, preferred_element_type=jnp.float32)
    acc_step = jnp.dot(activations, piece_step, preferred_element_type=jnp.float32)
    groups_in = acc_groups.astype(jnp.bfloat16)
    inner_in = acc_inner.astype(jnp.bfloat16)
    gate_in = acc_gate.astype(jnp.bfloat16)
    own_out_rows = lax.all_to_all(piece_out, "hid", split_axis=0, concat_axis=1, tiled=True)
    conv_group = lax.dynamic_slice_in_dim(conv_groups, group_index * group_cols, group_cols, 1)
    tail_rows = K - 1
    inner_prev, groups_prev = from_behind(
        (inner_in[tok_rows - tail_rows :], groups_in[tok_rows - tail_rows :]), "seq", 1
    )
    inner_conv = causal_conv(inner_in, inner_prev, conv_inner)
    groups_conv = causal_conv(groups_in, groups_prev, conv_group)
    step_size = jax.nn.softplus(acc_step + step_bias)
    rates = -jnp.exp(decay_log)
    span_count = tok_rows // Q
    heads_x = inner_conv.reshape(span_count, Q, heads_dev, P_SIZE)
    b_in = groups_conv[:, :N].reshape(span_count, Q, N)
    c_out = groups_conv[:, N:].reshape(span_count, Q, N)
    block_dt = step_size.reshape(span_count, Q, heads_dev)
    cum_decay = jnp.cumsum(block_dt * rates, axis=1)
    scores = jnp.einsum("ctn,csn->cts", c_out, b_in, preferred_element_type=jnp.float32)
    ahead = jnp.arange(Q)[:, None] >= jnp.arange(Q)[None, :]
    decay_t = jnp.swapaxes(cum_decay, 1, 2)
    gap = jnp.where(ahead, decay_t[:, :, :, None] - decay_t[:, :, None, :], -1e30)
    mixing = (scores[:, None] * jnp.exp(gap) * jnp.swapaxes(block_dt, 1, 2)[:, :, None, :]).astype(
        jnp.bfloat16
    )
    intra = jnp.einsum("chts,cshp->cthp", mixing, heads_x, preferred_element_type=jnp.float32)
    span_total = cum_decay[:, -1]
    weights_in = jnp.exp(span_total[:, None, :] - cum_decay) * block_dt
    weighted = (b_in[:, :, None, :] * weights_in[:, :, :, None]).astype(jnp.bfloat16)
    fresh = jnp.einsum("cshn,cshp->chnp", weighted, heads_x, preferred_element_type=jnp.float32)
    zero_state = jnp.zeros((heads_dev, N, P_SIZE), jnp.float32)
    local_end, starts = lax.scan(roll_state, zero_state, (span_total, fresh))
    log_total = jnp.sum(span_total, axis=0)
    prior = jnp.cumsum(span_total, axis=0) - span_total
    identity = (jnp.ones((heads_dev,), jnp.float32), zero_state)
    state_in = carried_in((jnp.exp(log_total), local_end), "seq", combine_states, identity)[1]
    span_in = starts + jnp.exp(prior)[:, :, None, None] * state_in[None]
    inter = jnp.einsum(
        "ctn,chnp->cthp", c_out.astype(jnp.float32), span_in, precision=lax.Precision.HIGHEST
    )
    inter = inter * jnp.exp(cum_decay)[:, :, :, None]
    mixed = (intra + inter).reshape(tok_rows, width_dev) + jnp.repeat(
        skip_gain, P_SIZE
    ) * inner_conv.astype(jnp.float32)
    gated = mixed * jax.nn.silu(gate_in.astype(jnp.float32))
    squares = lax.psum(jnp.sum(gated * gated, axis=1), "hid")
    normed = (gated * lax.rsqrt(squares / INNER + 1e-05)[:, None] * norm_gain).astype(jnp.bfloat16)
    start_sum = jnp.zeros((tok_rows, own_out_rows.shape[0]), jnp.float32)
    total = start_sum
    piece = lax.all_gather(normed, "hid", axis=1, tiled=True)
    block_count = piece.shape[1] // width_dev
    for block in range(block_count):
        cols = piece[:, block * width_dev : (block + 1) * width_dev]
        weight_cols = lax.dynamic_slice_in_dim(own_out_rows, block * width_dev, width_dev, 1)
        partial_out = lax.dot_general(
            cols, weight_cols, (((1,), (1,)), ((), ())), preferred_element_type=jnp.float32
        )
        total = total + lax.optimization_barrier(partial_out.astype(jnp.bfloat16)).astype(
            jnp.float32
        )
    return total.astype(jnp.bfloat16)


CORES = 2
HALO = 16
LANES = 128
VMEM = 36 * 1024 * 1024
COST = pl.CostEstimate(flops=1, bytes_accessed=1, transcendentals=0)


def both_cores(moves):
    return [(CORES * a + c, CORES * b + c) for a, b in moves for c in range(CORES)]


INWARD = both_cores([(0, 1), (3, 2)])
OUTWARD = both_cores([(1, 0), (2, 3)])
MIDDLE = both_cores([(1, 2), (2, 1)])
MIDDLE_UP = both_cores([(1, 2)])
NEAR = INWARD + OUTWARD


def other_core(block):
    return lax.ppermute(block, "seq", [(i, i ^ 1) for i in range(lax.axis_size("seq"))])


def along(block, route):
    return lax.ppermute(block, "seq", route)


def across(block, flip):
    return lax.ppermute(block, "hid", [(i, i ^ flip) for i in range(lax.axis_size("hid"))])


def silu(v):
    return v / (1.0 + jnp.exp(-v))


def convolved(window, taps, rows):
    summed = window[HALO : HALO + rows] * taps[K - 1 : K]
    for position in range(K - 1):
        shifted = pltpu.roll(window, K - 1 - position, 0)
        summed = summed + shifted[HALO : HALO + rows] * taps[position : position + 1]
    return silu(summed).astype(jnp.bfloat16)


def pair_of(low_half, left, right):
    return jnp.where(low_half, left, right)


def scan_kernel(
    first_ref, step_ref, taps_ref, group_taps_ref, bias_ref, decay_ref, skip_ref,
    y_ref, c_ref, grown_ref, end_ref, through_ref, prior_ref,
):
    span = pl.program_id(0)
    f32, bf16 = jnp.float32, jnp.bfloat16
    exact = lax.Precision.HIGHEST
    half = Q // 2

    @pl.when(span == 0)
    def _():
        end_ref[...] = jnp.zeros_like(end_ref)
        prior_ref[...] = jnp.zeros_like(prior_ref)

    width = y_ref.shape[1]
    rows = pl.ds(pl.multiple_of(span * Q, Q), Q + HALO)
    rounded = lambda columns: first_ref[rows, columns].astype(f32)
    groups = convolved(rounded(slice(width, width + 2 * N)), group_taps_ref[...], Q)
    b_in, c_out = groups[:, :N], groups[:, N:]
    c_ref[...] = c_out
    scores = lax.dot_general(c_out, b_in, (((1,), (1,)), ((), ())), preferred_element_type=f32)
    t_at = lax.broadcasted_iota(jnp.int32, (Q, Q), 0)
    s_at = lax.broadcasted_iota(jnp.int32, (Q, Q), 1)
    ahead = t_at >= s_at
    scores = jnp.where(ahead, scores, 0.0)
    raw = step_ref[...] + bias_ref[...]
    step = jnp.maximum(raw, 0.0) + jnp.log1p(jnp.exp(-jnp.abs(raw)))
    rated = step * -jnp.exp(decay_ref[...])
    cum = jnp.dot(jnp.where(ahead, 1.0, 0.0), rated, precision=exact, preferred_element_type=f32)
    last = cum[Q - 1 : Q, :]
    prior = prior_ref[...]
    grown_ref[...] = jnp.exp(cum + prior)
    prior_ref[...] = prior + last
    through = jnp.exp(prior + last)
    cum_t, step_t = cum.T, step.T
    grow = jnp.exp(cum)
    weight = jnp.exp(last - cum) * step
    fade = jnp.exp(last)
    low = lax.broadcasted_iota(jnp.int32, (Q, LANES), 1) < P_SIZE
    per = LANES // P_SIZE
    for j in range(width // LANES):
        lanes = slice(j * LANES, (j + 1) * LANES)
        x = convolved(rounded(lanes), taps_ref[:, lanes], Q)
        x_wide = x.astype(f32)
        parts = []
        for h in (per * j, per * j + 1):
            col = cum[:, h : h + 1]
            row, scale = cum_t[h : h + 1, :], step_t[h : h + 1, :]
            top = scores[:half, :half] * jnp.exp(jnp.minimum(col[:half] - row[:, :half], 0.0)) * scale[:, :half]
            bottom = scores[half:] * jnp.exp(jnp.minimum(col[half:] - row, 0.0)) * scale
            parts.append(
                jnp.concatenate(
                    [
                        jnp.dot(top.astype(bf16), x[:half], preferred_element_type=f32),
                        jnp.dot(bottom.astype(bf16), x, preferred_element_type=f32),
                    ],
                    axis=0,
                )
            )
        y = pair_of(low, parts[0], parts[1])
        a, b = per * j, per * j + 1
        state = end_ref[:, lanes]
        high = state.astype(bf16)
        rest = (state - high.astype(f32)).astype(bf16)
        carried = jnp.dot(c_out, high, preferred_element_type=f32) + jnp.dot(c_out, rest, preferred_element_type=f32)
        y = y + carried * pair_of(low, grow[:, a : a + 1], grow[:, b : b + 1])
        y_ref[:, lanes] = y + x_wide * skip_ref[:, lanes]
        weighted = (x_wide * pair_of(low, weight[:, a : a + 1], weight[:, b : b + 1])).astype(bf16)
        fresh = lax.dot_general(b_in, weighted, (((0,), (0,)), ((), ())), preferred_element_type=f32)
        end_ref[:, lanes] = state * pair_of(low[:1], fade[:, a : a + 1], fade[:, b : b + 1]) + fresh
        through_ref[:, lanes] = pair_of(low[:1], through[:, a : a + 1], through[:, b : b + 1])


def scan_segment(first, step, taps, group_taps, bias, decay, skip):
    tokens, width = step.shape[0], taps.shape[1]
    whole = lambda a: pl.BlockSpec(a.shape, lambda i: (0,) * a.ndim)
    spans = lambda w: pl.BlockSpec((Q, w), lambda i: (i, 0))
    fixed = lambda shape: pl.BlockSpec(shape, lambda i: (0, 0))
    f32 = jnp.float32
    return pl.pallas_call(
        scan_kernel,
        grid=(tokens // Q,),
        in_specs=[whole(first), spans(LANES)] + [whole(a) for a in (taps, group_taps, bias, decay, skip)],
        out_specs=[spans(width), spans(N), spans(LANES), fixed((N, width)), fixed((1, width))],
        out_shape=[
            jax.ShapeDtypeStruct((tokens, width), f32),
            jax.ShapeDtypeStruct((tokens, N), jnp.bfloat16),
            jax.ShapeDtypeStruct((tokens, LANES), f32),
            jax.ShapeDtypeStruct((N, width), f32),
            jax.ShapeDtypeStruct((1, width), f32),
        ],
        scratch_shapes=[pltpu.VMEM((1, LANES), f32)],
        compiler_params=pltpu.CompilerParams(vmem_limit_bytes=VMEM),
        cost_estimate=COST,
        name="scan_segment",
    )(first, step, taps, group_taps, bias, decay, skip)


def fetch(at_ref, sources, pieces, source_buf, piece_buf, sems):
    rows = piece_buf.shape[1]
    each = source_buf.shape[1] // len(sources)
    waits = []
    for piece in pieces:
        for part in range(piece.shape[0] // rows):
            i = len(waits)
            columns = pl.ds(pl.multiple_of(at_ref[i] * rows, rows), rows)
            copies = [pltpu.make_async_copy(piece.at[pl.ds(part * rows, rows)], piece_buf.at[i], sems.at[i, 0])]
            for k, source in enumerate(sources):
                first = source.shape[0] - each
                copies.append(
                    pltpu.make_async_copy(
                        source.at[pl.ds(first, each), columns], source_buf.at[i, pl.ds(k * each, each)], sems.at[i, 1 + k]
                    )
                )
            for copy in copies:
                copy.start()
            waits.append(lambda copies=copies: [copy.wait() for copy in copies])
    return waits


def blocks_of(width):
    step = 2 * LANES
    return [slice(n, min(n + step, width)) for n in range(0, width, step)]


def project_kernel(n_sources, count, begun, final, at_ref, *refs):
    sources, pieces, refs = refs[:n_sources], refs[n_sources : n_sources + count], refs[n_sources + count :]
    partial_ref, refs = (refs[0], refs[1:]) if begun else (None, refs)
    outs, (total_ref, source_buf, piece_buf, sems) = refs[:-4], refs[-4:]
    waits = fetch(at_ref, sources, pieces, source_buf, piece_buf, sems)
    for i in range(0, len(waits), 2):
        waits[i]()
        waits[i + 1]()
        for columns in blocks_of(total_ref.shape[1]):
            term = jnp.dot(source_buf[i], piece_buf[i, :, columns], preferred_element_type=jnp.float32)
            term = term + jnp.dot(source_buf[i + 1], piece_buf[i + 1, :, columns], preferred_element_type=jnp.float32)
            if i or begun:
                term = term + (total_ref if i else partial_ref)[:, columns]
            total_ref[:, columns] = term
    if final:
        outs[0][...] = total_ref[:, : outs[0].shape[1]].astype(outs[0].dtype)
        outs[1][...] = total_ref[HALO:, outs[0].shape[1] :]


def project(sources, tokens, pieces, places, rows, partial=None, final=False):
    steps, width = places.shape[0], pieces[0].shape[1]
    height = tokens * len(sources)
    f32 = jnp.float32
    if final:
        out_shape = [
            jax.ShapeDtypeStruct((height, width - LANES), jnp.bfloat16),
            jax.ShapeDtypeStruct((height - HALO, LANES), f32),
        ]
    else:
        out_shape = jax.ShapeDtypeStruct((height, width), f32)
    total = [pltpu.VMEM((height, width), f32)] if final else []
    kernel = functools.partial(project_kernel, len(sources), len(pieces), partial is not None, final)

    def body(*refs):
        if final:
            kernel(*refs)
        else:
            kernel(*refs[:-4], *refs[-4:])

    vmem = pl.BlockSpec(memory_space=pltpu.VMEM)
    return pl.pallas_call(
        body,
        in_specs=[pl.BlockSpec(memory_space=pltpu.SMEM)]
        + [pl.BlockSpec(memory_space=pl.ANY)] * (len(sources) + len(pieces))
        + ([vmem] if partial is not None else []),
        out_specs=[vmem] * 2 if final else vmem,
        out_shape=out_shape,
        scratch_shapes=total
        + [
            pltpu.VMEM((steps, height, rows), jnp.bfloat16),
            pltpu.VMEM((steps, rows, width), jnp.bfloat16),
            pltpu.SemaphoreType.DMA((steps, 1 + len(sources))),
        ],
        compiler_params=pltpu.CompilerParams(vmem_limit_bytes=VMEM),
        cost_estimate=COST,
        name="project",
    )(places, *sources, *pieces, *([partial] if partial is not None else []))


def two_rows(row, height):
    high = row.astype(jnp.bfloat16).astype(jnp.float32)
    at = lax.broadcasted_iota(jnp.int32, (height, row.shape[1]), 0)
    return jnp.where(at == 0, high, jnp.where(at == 1, row - high, 0.0)).astype(jnp.bfloat16)


def gate_kernel(count, at_ref, source_ref, *refs):
    pieces, refs = refs[:count], refs[count:]
    begun_ref, y_ref, c_ref, grown_ref, state_ref, gain_ref, *outs, source_buf, piece_buf, sems = refs
    f32, bf16 = jnp.float32, jnp.bfloat16
    waits = fetch(at_ref, [source_ref], pieces, source_buf, piece_buf, sems)
    c_out, grown = c_ref[...], grown_ref[...]
    grown_high = grown.astype(bf16)
    grown_rest = (grown - grown_high.astype(f32)).astype(bf16)
    squares = None
    share = y_ref.shape[0] // len(outs)
    for n, columns in enumerate(blocks_of(y_ref.shape[1])):
        block = columns.stop - columns.start
        total = begun_ref[:, columns]
        for i in range(len(waits)):
            if n == 0:
                waits[i]()
            total = total + jnp.dot(source_buf[i], piece_buf[i, :, columns], preferred_element_type=f32)
        lane = lax.broadcasted_iota(jnp.int32, (LANES, block), 1) + columns.start
        of_head = jnp.where(lane // P_SIZE == lax.broadcasted_iota(jnp.int32, (LANES, block), 0), 1.0, 0.0).astype(bf16)
        spread = jnp.dot(grown_high, of_head, preferred_element_type=f32)
        spread = spread + jnp.dot(grown_rest, of_head, preferred_element_type=f32)
        state = state_ref[:, columns]
        high = state.astype(bf16)
        rest = (state - high.astype(f32)).astype(bf16)
        carried = jnp.dot(c_out, high, preferred_element_type=f32) + jnp.dot(c_out, rest, preferred_element_type=f32)
        gated = (y_ref[:, columns] + carried * spread) * silu(total.astype(bf16).astype(f32))
        scaled = (gated * gain_ref[:, columns]).astype(bf16)
        for k, out in enumerate(outs):
            out[:share, columns] = scaled[k * share : (k + 1) * share]
        square = gated * gated
        for k in range(block // LANES):
            part = square[:, k * LANES : (k + 1) * LANES]
            squares = part if squares is None else squares + part
    ones = jnp.ones((8, LANES), f32)
    for k, out in enumerate(outs):
        part = squares[k * share : (k + 1) * share]
        row = lax.dot_general(
            ones, part, (((1,), (1,)), ((), ())), precision=lax.Precision.HIGHEST, preferred_element_type=f32
        )[:1]
        row = jnp.concatenate([row, jnp.zeros((1, out.shape[1] - share), f32)], axis=1)
        out[share:] = two_rows(row, out.shape[0] - share)


def gate_with(source, pieces, places, begun, part, scanned, state, gain, parts):
    y, c_out, grown = scanned
    tokens, width = y.shape
    steps = places.shape[0]
    rows = sum(piece.shape[0] for piece in pieces) // steps
    vmem = pl.BlockSpec(memory_space=pltpu.VMEM)
    return pl.pallas_call(
        functools.partial(gate_kernel, len(pieces)),
        grid=(1,),
        in_specs=[pl.BlockSpec(memory_space=pltpu.SMEM)]
        + [pl.BlockSpec(memory_space=pl.ANY)] * (1 + len(pieces))
        + [pl.BlockSpec((tokens, width), lambda i: (part, 0))]
        + [vmem] * 5,
        out_specs=[vmem] * parts,
        out_shape=[jax.ShapeDtypeStruct((tokens // parts + HALO, width), jnp.bfloat16)] * parts,
        scratch_shapes=[
            pltpu.VMEM((steps, tokens, rows), jnp.bfloat16),
            pltpu.VMEM((steps, rows, width), jnp.bfloat16),
            pltpu.SemaphoreType.DMA((steps, 2)),
        ],
        compiler_params=pltpu.CompilerParams(vmem_limit_bytes=VMEM),
        cost_estimate=COST,
        name="gate",
    )(places, source, *pieces, begun, y, c_out, grown, state, gain[None, :])


def output_kernel(at_ref, here_ref, back_ref, *refs):
    weights, outs, (block_buf, weight_buf, sems) = refs[:4], refs[4:-3], refs[-3:]
    features = weight_buf.shape[1]
    tokens = block_buf.shape[0] - HALO
    here = pltpu.make_async_copy(here_ref, block_buf, sems.at[2 * len(outs)])
    back = pltpu.make_async_copy(back_ref, block_buf, sems.at[2 * len(outs)])
    stays = at_ref[len(outs)] == 1
    pl.when(stays)(here.start)
    pl.when(jnp.logical_not(stays))(back.start)
    waits = []
    for j in range(len(outs)):
        for i in range(2):
            slot = 2 * j + i
            index, is_near = at_ref[j] % 2, at_ref[j] < 2
            near, far = [pltpu.make_async_copy(weights[k + i].at[index], weight_buf.at[slot], sems.at[slot]) for k in (0, 2)]
            pl.when(is_near)(near.start)
            pl.when(jnp.logical_not(is_near))(far.start)
            waits.append((is_near, near, far))
    pl.when(stays)(here.wait)
    pl.when(jnp.logical_not(stays))(back.wait)
    for j, out in enumerate(outs):
        out[tokens:] = block_buf[tokens:]
        for i in range(2):
            is_near, near, far = waits[2 * j + i]
            pl.when(is_near)(near.wait)
            pl.when(jnp.logical_not(is_near))(far.wait)
            product = lax.dot_general(
                block_buf[:tokens], weight_buf[2 * j + i], (((1,), (1,)), ((), ())), preferred_element_type=jnp.float32
            )
            out[:tokens, i * features : (i + 1) * features] = product.astype(out.dtype)


def output_parts(here, back, pairs, at):
    height, width = here.shape
    features, count = pairs[0].shape[1], at.shape[0] - 1
    vmem, anywhere = pl.BlockSpec(memory_space=pltpu.VMEM), pl.BlockSpec(memory_space=pl.ANY)
    return pl.pallas_call(
        output_kernel,
        in_specs=[pl.BlockSpec(memory_space=pltpu.SMEM)] + [anywhere] * 6,
        out_specs=[vmem] * count,
        out_shape=[jax.ShapeDtypeStruct((height, 2 * features), jnp.bfloat16)] * count,
        scratch_shapes=[
            pltpu.VMEM((height, width), jnp.bfloat16),
            pltpu.VMEM((2 * count, features, width), jnp.bfloat16),
            pltpu.SemaphoreType.DMA((2 * count + 1,)),
        ],
        compiler_params=pltpu.CompilerParams(vmem_limit_bytes=VMEM),
        cost_estimate=COST,
        name="output_parts",
    )(at, here, back, *pairs)


def pack_kernel(at_ref, mine_ref, lent_ref, mine_fade_ref, lent_fade_ref, out_ref):
    lent_first = at_ref[at_ref.shape[0] - 1] == 1
    for which in range(2):
        pick = lent_first if which == 0 else jnp.logical_not(lent_first)
        out_ref[which, :N] = jnp.where(pick, lent_ref[...], mine_ref[...]).astype(out_ref.dtype)
        out_ref[which, N:] = two_rows(jnp.where(pick, lent_fade_ref[...], mine_fade_ref[...]), out_ref.shape[1] - N)


def segments_of(at_ref, own_ref, other_ref):
    core = at_ref[at_ref.shape[0] - 2]
    for which in range(2):
        for c in range(CORES):
            read = lambda rows: jnp.where(
                core == c, own_ref[which, rows].astype(jnp.float32), other_ref[which, rows].astype(jnp.float32)
            )
            fade = read(slice(N, N + HALO))
            yield which, c, fade[:1] + fade[1:2], read(slice(0, N))


def through_kernel(at_ref, own_ref, other_ref, out_ref):
    state = None
    for _, _, fade, end in segments_of(at_ref, own_ref, other_ref):
        state = end if state is None else fade * state + end
    out_ref[...] = state.astype(out_ref.dtype)


def starts_kernel(at_ref, own_ref, other_ref, before_ref, mine_ref, lent_ref):
    lent_first, core = at_ref[at_ref.shape[0] - 1] == 1, at_ref[at_ref.shape[0] - 2]
    state = before_ref[...].astype(jnp.float32)
    for which, c, fade, end in segments_of(at_ref, own_ref, other_ref):
        to_lent = lent_first if which == 0 else jnp.logical_not(lent_first)

        @pl.when((core == c) & to_lent)
        def _(state=state):
            lent_ref[...] = state

        @pl.when((core == c) & jnp.logical_not(to_lent))
        def _(state=state):
            mine_ref[...] = state

        state = fade * state + end


def on_states(kernel, shapes, at, *arrays):
    vmem = pl.BlockSpec(memory_space=pltpu.VMEM)
    return pl.pallas_call(
        kernel,
        in_specs=[pl.BlockSpec(memory_space=pltpu.SMEM)] + [vmem] * len(arrays),
        out_specs=[vmem] * len(shapes),
        out_shape=shapes,
        compiler_params=pltpu.CompilerParams(vmem_limit_bytes=VMEM),
        cost_estimate=COST,
        name="states",
    )(at, *arrays)


def arrange_kernel(moves, count, at_ref, *refs):
    sources, outs, sems = refs[:count], refs[count:-1], refs[-1]
    copies = []
    for k, (source, rows, out, place, condition) in enumerate(moves):
        copy = pltpu.make_async_copy(sources[source].at[rows], outs[out].at[place(at_ref)], sems.at[k])
        copies.append((copy, condition))
    for copy, condition in copies:
        copy.start() if condition is None else pl.when(condition(at_ref))(copy.start)
    for copy, condition in copies:
        copy.wait() if condition is None else pl.when(condition(at_ref))(copy.wait)


def arrange(sources, shapes, moves, at):
    anywhere = pl.BlockSpec(memory_space=pl.ANY)
    return pl.pallas_call(
        functools.partial(arrange_kernel, moves, len(sources)),
        in_specs=[pl.BlockSpec(memory_space=pltpu.SMEM)] + [anywhere] * len(sources),
        out_specs=[pl.BlockSpec(memory_space=pltpu.VMEM)] * len(shapes),
        out_shape=[jax.ShapeDtypeStruct(shape, sources[0].dtype) for shape in shapes],
        scratch_shapes=[pltpu.SemaphoreType.DMA((len(moves),))],
        compiler_params=pltpu.CompilerParams(vmem_limit_bytes=VMEM),
        cost_estimate=COST,
        name="arrange",
    )(at, *sources)


def stacked(blocks, at):
    moves, first = [], 0
    for k, block in enumerate(blocks):
        rows = slice(first, first + block.shape[0])
        moves.append((k, slice(None), 0, lambda at_ref, rows=rows: rows, None))
        first = rows.stop
    return arrange(blocks, [(first,) + blocks[0].shape[1:]], moves, at)[0]


class Order:
    def __init__(self, token):
        self.token = token

    def wait(self, *blocks):
        self.token, *blocks = lax.optimization_barrier((self.token, *blocks))
        return blocks[0] if len(blocks) == 1 else blocks

    def now(self, block):
        return lax.optimization_barrier((block, self.token))[0]


def local_paired(
    activations, w_inner, w_gate, w_groups, w_step, w_out, conv_inner, conv_groups, step_bias, decay_log, skip_gain, norm_gain
):
    f32, bf16 = jnp.float32, jnp.bfloat16
    tokens, depth = activations.shape
    heads_dev = step_bias.shape[0]
    width = w_inner.shape[1]
    place, head_block = lax.axis_index("seq"), lax.axis_index("hid")
    plane, core = place // CORES, place % CORES
    lower = plane < 2
    middle = (plane == 1) | (plane == 2)
    group_cols = 2 * N
    group_index = head_block * heads_dev // (HEADS // G)
    pad = LANES - heads_dev
    devices, chips = lax.axis_size("seq"), lax.axis_size("hid")
    half = tokens // 2
    order = Order(step_bias)
    now, wait = order.now, order.wait

    kept_tokens = K
    folded = activations[tokens - kept_tokens :].reshape(HALO, kept_tokens * depth // HALO)
    w_first = jnp.concatenate(
        [
            w_inner,
            lax.dynamic_slice_in_dim(w_groups, group_index * group_cols, group_cols, 1),
            jnp.pad(lax.dynamic_slice_in_dim(w_step, head_block * heads_dev, heads_dev, 1), ((0, 0), (0, pad))),
        ],
        axis=1,
    )
    w_first = jnp.concatenate([w_first, jnp.pad(folded, ((0, 0), (0, w_first.shape[1] - folded.shape[1])))], axis=0)
    tail_of = lambda block: block[block.shape[0] - HALO :, : folded.shape[1]]
    unfolded = lambda tail: jnp.pad(tail.reshape(kept_tokens, depth), ((HALO - kept_tokens, 0), (0, 0)))
    quarter = depth // chips

    mirrored = chips - 1 - plane
    partner = plane ^ 1
    places_of = lambda *planes: jnp.stack([jnp.clip(p, 0, chips - 1) * CORES + c for p in planes for c in (core, 1 - core)])
    early, late = places_of(plane, mirrored), places_of(partner, mirrored ^ 1)
    group_taps = lax.dynamic_slice_in_dim(conv_groups, group_index * group_cols, group_cols, 1)
    lane_row = lambda v: jnp.pad(v, (0, pad))[None, :]
    consts = (conv_inner, group_taps, lane_row(step_bias), lane_row(decay_log), jnp.repeat(skip_gain, P_SIZE)[None, :])
    rows = w_out.shape[0]
    to = jnp.stack([head_block ^ flip for flip in range(chips)] + [middle.astype(jnp.int32), core, lower.astype(jnp.int32)])
    first_out, first_far = along(w_first, INWARD), along(w_first, MIDDLE)
    lent = lax.dynamic_slice_in_dim(activations, head_block * quarter, quarter, 1)
    first_x, gate_x, lent = wait(other_core(w_first), other_core(w_gate), lent)
    lent_here = along(now(lent), INWARD)
    first_far, first_out = wait(first_far, first_out)
    first_end, near = along(now(first_out), MIDDLE), along(now(w_out), NEAR)
    far_x, out_x = wait(other_core(now(first_far)), other_core(now(first_out)))
    tail_x, tail_far, tail_out = tail_of(first_x), tail_of(far_x), tail_of(out_x)
    halo = unfolded(jnp.where(core == 1, tail_x, jnp.where(plane == 1, tail_out, tail_far)))
    halo_lent = unfolded(jnp.where(core == 1, tail_out, jnp.where(plane == 1, jnp.zeros_like(tail_x), tail_x)))
    mine, halo_lent = wait(stacked([halo, activations], now(to)), halo_lent)
    first_early = [w_first, first_x, first_far, far_x]
    begun_mine, lent_here = wait(project([mine], tokens + HALO, first_early, now(early), rows), lent_here)
    lent_x, lent_y, out_far = across(now(lent_here), 1), across(now(lent_here), 2), along(now(w_out), MIDDLE)
    first_end, near, lent_x, lent_y, out_far = wait(first_end, near, lent_x, lent_y, out_far)
    end_x, out_end = other_core(now(first_end)), along(now(near), MIDDLE)
    by_x, by_y = wait(
        *arrange(
            [lent_y, lent_x],
            [(half, quarter), (tokens - half, quarter)],
            [
                (0, slice(0, half), 0, lambda at: slice(None), None),
                (1, slice(half, tokens), 1, lambda at: slice(None), None),
            ],
            now(to),
        )
    )
    by_x, by_y = across(now(by_x), 1), across(now(by_y), 2)
    end_x = wait(end_x)
    gate_far, out_far_on = along(now(w_gate), MIDDLE), along(now(out_far), OUTWARD)
    first_late = [first_out, out_x, first_end, end_x]
    first_mine, step_mine, by_x, by_y = wait(
        *project([mine], tokens + HALO, first_late, now(late), rows, begun_mine, True), by_x, by_y
    )
    gate_out = along(now(w_gate), INWARD)
    columns = lambda flip, first, last: lambda at: (slice(HALO + first, HALO + last), pl.ds(at[flip] * quarter, quarter))
    (borrowed,) = arrange(
        [halo_lent, lent_here, lent_x, lent_y, by_x, by_y],
        [(HALO + tokens, depth)],
        [(0, slice(None), 0, lambda at: slice(0, HALO), None)]
        + [(1 + flip, slice(None), 0, columns(flip, 0, tokens), None) for flip in range(3)]
        + [(4, slice(None), 0, columns(3, 0, half), None), (5, slice(None), 0, columns(3, half, tokens), None)],
        now(to),
    )
    borrowed = wait(borrowed)
    first_lent, step_lent = wait(
        *project([borrowed], tokens + HALO, first_early + first_late, now(jnp.concatenate([early, late])), rows, None, True)
    )
    scanned_lent, end_lent, through_lent = split_scan(wait(*scan_segment(now(first_lent), step_lent, *consts)))
    out_end, gate_out, gate_far, out_far_on = wait(out_end, gate_out, gate_far, out_far_on)
    out_end_on, gate_end = along(now(out_end), OUTWARD), along(now(gate_out), MIDDLE)
    gate_out_x, gate_far_x = other_core(now(gate_out)), other_core(now(gate_far))
    scanned_mine, end_mine, through_mine = split_scan(wait(*scan_segment(now(first_mine), step_mine, *consts)))

    state = jax.ShapeDtypeStruct((N, width), f32)
    (ends,) = on_states(
        pack_kernel, [jax.ShapeDtypeStruct((2, N + HALO, width), bf16)], now(to), end_mine, end_lent, through_mine, through_lent
    )
    ends = wait(ends)
    ends_other = wait(other_core(now(ends)))
    (run,) = wait(on_states(through_kernel, [jax.ShapeDtypeStruct((N, width), bf16)], now(to), ends, ends_other))
    state_in = along(now(run), MIDDLE_UP)
    gate_out_x, gate_far_x = wait(gate_out_x, gate_far_x)
    gate_early = [w_gate, gate_x, gate_out, gate_out_x, gate_far, gate_far_x]
    gate_begun = wait(project([borrowed, mine], tokens, gate_early, now(places_of(plane, partner, mirrored)), rows))
    gate_end, state_in, out_end_on = wait(gate_end, state_in, out_end_on)
    gate_end_x = other_core(now(gate_end))
    row = lambda index: lambda at: slice(index * rows, (index + 1) * rows)
    stays, goes = lambda at: at[chips] == 1, lambda at: at[chips] == 0
    both, far = wait(
        *arrange(
            [w_out, near, out_far, out_end, out_far_on, out_end_on],
            [(2 * rows, width)] * 2,
            [
                (0, slice(None), 0, row(0), None),
                (1, slice(None), 0, row(1), None),
                (2, slice(None), 1, row(0), stays),
                (3, slice(None), 1, row(1), stays),
                (4, slice(None), 1, row(0), goes),
                (5, slice(None), 1, row(1), goes),
            ],
            now(to),
        )
    )
    state_mine, state_lent, gate_end_x = wait(
        *on_states(starts_kernel, [state] * 2, now(to), ends, ends_other, state_in), gate_end_x
    )
    both_x, far_x = other_core(now(both)), other_core(now(far))
    gate_rest, there = [gate_end, gate_end_x], places_of(mirrored ^ 1)

    count = 2
    lent_parts = wait(*gate_with(borrowed, gate_rest, now(there), gate_begun, 0, scanned_lent, state_lent, norm_gain, count))
    backs = [along(now(part), OUTWARD) for part in lent_parts]
    mine_parts = wait(*gate_with(mine, gate_rest, now(there), gate_begun, 1, scanned_mine, state_mine, norm_gain, count))
    back0, far_x, both_x = wait(backs[0], far_x, both_x)
    pairs = [block.reshape(2, rows, width) for block in (both, both_x, far, far_x)]
    place_of = lambda index: jnp.where(
        index == plane, 0, jnp.where(index == partner, 1, jnp.where(index == jnp.where(lower, 2, 1), 2, 3))
    )

    def products_of(part, back, *flips):
        at = jnp.stack([place_of(head_block ^ flip) for flip in flips] + [middle.astype(jnp.int32)])
        return wait(*output_parts(mine_parts[part], back, pairs, now(at)))

    by3, by1, by2, top = products_of(0, back0, 3, 1, 2, 0)
    sent3, sent1, sent2 = across(now(by3), 3), across(now(by1), 1), across(now(by2), 2)
    back1 = wait(backs[1])
    by3, by1, by2, bottom = products_of(1, back1, 3, 1, 2, 0)
    sent3 = wait(sent3)
    next3 = across(now(by3), 3)
    sent1, sent2 = wait(sent1, sent2)
    next1, next2 = across(now(by1), 1), across(now(by2), 2)
    result = wait(sum_part([top, sent1, sent2, sent3], 0, count, to))
    return sum_part([bottom, next1, next2, next3], 1, count, now(to), result)


def sum_kernel(at_ref, *refs):
    blocks, out_ref = refs[:4], refs[-1]
    tokens, width = out_ref.shape
    f32 = jnp.float32
    squares = sum(block[tokens:].astype(f32) for block in blocks)
    row = (squares[:1] + squares[1:2])[:, :tokens]
    norm = lax.rsqrt(row / INNER + 1e-05)
    norm = jnp.broadcast_to(norm, (LANES, tokens)).T[:, :1]
    own_first = at_ref[at_ref.shape[0] - 2] == 0
    half = width // 2
    low, high = [
        sum(block[:tokens, columns].astype(f32) for block in blocks) * norm for columns in (slice(0, half), slice(half, width))
    ]
    out_ref[:, :half] = jnp.where(own_first, low, high).astype(out_ref.dtype)
    out_ref[:, half:] = jnp.where(own_first, high, low).astype(out_ref.dtype)


def sum_part(blocks, part, count, at, result=None):
    height, width = blocks[0].shape
    tokens = height - HALO
    vmem = pl.BlockSpec(memory_space=pltpu.VMEM)
    return pl.pallas_call(
        sum_kernel,
        grid=(1,),
        in_specs=[pl.BlockSpec(memory_space=pltpu.SMEM)]
        + [vmem] * len(blocks)
        + ([pl.BlockSpec(memory_space=pl.ANY)] if part else []),
        out_specs=pl.BlockSpec((tokens, width), lambda i: (part, 0)),
        out_shape=jax.ShapeDtypeStruct((tokens * count, width), jnp.bfloat16),
        input_output_aliases={1 + len(blocks): 0} if part else {},
        compiler_params=pltpu.CompilerParams(vmem_limit_bytes=VMEM),
        cost_estimate=pl.CostEstimate(flops=1, bytes_accessed=32 * tokens * width * count, transcendentals=0),
        name="sum_part",
    )(at, *blocks, *([result] if part else []))


def split_scan(results):
    return results[:3], results[3], results[4]


def plan_of(mesh):
    planes = mesh.shape["seq"] // CORES
    return local_paired if planes == 4 and mesh.shape["hid"] == planes else local_general


def solution(mesh):
    in_specs = (
        P("seq", None),
        P("seq", "hid"),
        P("seq", "hid"),
        P("seq", None),
        P("seq", None),
        P("seq", "hid"),
        P(None, "hid"),
        P(),
        P("hid"),
        P("hid"),
        P("hid"),
        P("hid"),
    )
    out_specs = P("seq", "hid")
    return jax.shard_map(plan_of(mesh), mesh=mesh, in_specs=in_specs, out_specs=out_specs, check_vma=False)
```
